128 devices in a mesh: row: 4 (over z), bulk: 32 (over y, x, core).
Axes of the slice: x: 4, y: 4, z: 4, core: 2. Of those that a mesh axis runs over, the one named last changes fastest.
Arguments:
- density: bfloat16 [96, 96, 128, 128], P('row', 'bulk'), may hold values from -6 to 6
- factors: bfloat16 [96, 384, 128], replicated, may hold values from -0.5 to 0.5
- core: float32 [384, 384], replicated, as said below
- task_blocks: int32 [128, 12], P(('row', 'bulk')), may hold values from 0 to 95, as said below
- quartets: int32 [16384, 4], P(('row', 'bulk')), may hold values from 0 to 11
- quartet_count: int32 [128], P(('row', 'bulk')), may hold values from 1 to 128, as said below
Outputs:
- fock: float32 [96, 96, 128, 128], P('row', 'bulk')
The draws below stay inside these ranges and needn't reach their ends.
Inputs may be any that keep to these rules, and one draw needn't show every extreme that they name: `task_blocks`: each row holds 12 distinct shell blocks: entries g * 3 to g * 3 + 2 lie in blocks g * 24 to g * 24 + 23, and no two entries of a row lie in the same aligned group of 3 blocks. `quartet_count`: some device has all 128 slots live, and another one has a single live slot. core[p, q] = core[q, p].
All inputs are finite; a program needn't handle non-finite values.
Results may differ from the reference program's by a relative error of at most 0.015.
Values may be sent and summed in bfloat16 or wider, within the bound.
A program may use at most 256 MiB of HBM per device.

```python
import math
import jax
import jax.numpy as jnp
from jax import lax

BS = 128
R = 384
NBC = 3
Q_DEV = 128
NB = 96
TASK_BLK = 12
CAP = 3
QUARTETS = 16384
N_ROW = 4
N_BULK = 32


def draw_task_blocks(key, part):
    key = jax.random.fold_in(key, 11)
    devs = N_ROW * N_BULK
    per_row = N_BULK // N_ROW
    score_key, within_key = jax.random.split(key)
    scores = jax.random.randint(score_key, (devs, N_ROW, per_row), 0, 1 << 20) * per_row + jnp.arange(per_row, dtype=jnp.int32)
    order = jnp.argsort(scores, axis=-1, stable=True)[:, :, :CAP].astype(jnp.int32)
    group = jnp.arange(N_ROW, dtype=jnp.int32)[None, :, None] * per_row + order
    within = jax.random.randint(within_key, (devs, N_ROW, CAP), 0, NBC)
    return (group * NBC + within).reshape(devs, TASK_BLK).astype(jnp.int32)


def draw_quartet_count(key, part):
    key = jax.random.fold_in(key, 23)
    devs = N_ROW * N_BULK
    shift_key, cut_key, pick_key, other_key = jax.random.split(key, 4)
    shifts = jax.random.randint(shift_key, (devs,), 0, 4)
    base = Q_DEV // jnp.power(2, shifts).astype(jnp.int32)
    cut = jax.random.randint(cut_key, (devs,), 0, base // 2 + 1)
    counts = base - cut
    chosen = jax.random.randint(pick_key, (), 0, devs)
    other = (chosen + 1 + jax.random.randint(other_key, (), 0, devs - 1)) % devs
    indices = jnp.arange(devs, dtype=jnp.int32)
    counts = jnp.where(indices == chosen, Q_DEV, counts)
    counts = jnp.where(indices == other, 1, counts)
    return counts.astype(jnp.int32)


def draw_core(key, part):
    key = jax.random.fold_in(key, 37)
    base = jax.random.normal(key, (R, R), jnp.float32)
    return ((base + base.T) * (2.4 / math.sqrt(2.0 * R))).astype(jnp.float32)


def set_ends(drawn, rng, low, largest):
    longest = drawn.shape.index(max(drawn.shape))
    spots = []
    for shift in (0, 1):
        where = [jax.random.randint(jax.random.fold_in(rng, axis), (), 0, length) for axis, length in enumerate(drawn.shape)]
        where[longest] = (where[longest] + shift) % drawn.shape[longest]
        spots.append(tuple(where))
    return drawn.at[spots[0]].set(low).at[spots[1]].set(largest)


def steps_of(rng, shape, cuts, smallest, largest):
    factor_of = 1.0
    for position, parts in cuts:
        draws = jax.random.uniform(jax.random.fold_in(jax.random.fold_in(rng, 6), position), (parts,), jnp.float32, smallest / len(cuts), largest / len(cuts))
        factor_of = factor_of * jnp.repeat(jnp.exp(draws), shape[position] // parts).reshape((-1,) + (1,) * (len(shape) - 1 - position))
    return factor_of


def normal_values(key, dims, spread, bound, cuts=(), kind=jnp.bfloat16):
    level = steps_of(key, dims, cuts, -0.22, 0.18) if cuts else 1.0
    array = jax.random.normal(key, dims, jnp.float32) * spread * level
    return jnp.minimum(jnp.maximum(array, -bound), bound).astype(kind)


def setup_inputs(seed: int = 0) -> dict:
    keys = jax.random.split(jax.random.key(seed), 7)
    return {
        "density": normal_values(keys[0], (NB, NB, BS, BS), 1.0, 6.0, ((0, 4), (1, 32))),
        "factors": normal_values(keys[1], (NB, R, BS), BS ** -0.5, 0.5),
        "core": draw_core(jax.random.fold_in(keys[6], 71), 0),
        "task_blocks": draw_task_blocks(jax.random.fold_in(keys[6], 71), 0),
        "quartets": set_ends(jax.random.randint(keys[4], (QUARTETS, 4), 0, TASK_BLK), jax.random.fold_in(keys[4], 1), 0, TASK_BLK - 1).astype(jnp.int32),
        "quartet_count": draw_quartet_count(jax.random.fold_in(keys[6], 71), 0),
    }


def rounded(value):
    return lax.optimization_barrier(value.astype(jnp.bfloat16)).astype(jnp.float32)


def device_piece(density, factors, core, blocks, quads, count):
    ntask = blocks.shape[0]
    npairs = ntask * ntask
    points = factors.shape[1]
    cache = density[blocks[:, None], blocks[None, :]].astype(jnp.float32)
    coef = factors[blocks].astype(jnp.float32)
    halfway = rounded(jnp.einsum("xpi,xyij->xypj", coef, cache))
    pairwise = rounded(jnp.einsum("xypj,yqj->xypq", halfway, coef))
    pair_diag = jnp.sum(halfway * coef[None], axis=-1)
    live = (jnp.arange(quads.shape[0], dtype=jnp.int32) < count).astype(jnp.float32)
    first = quads[:, 0]
    second = quads[:, 1]
    third = quads[:, 2]
    fourth = quads[:, 3]
    coulomb_coef = jnp.zeros((npairs, npairs), jnp.float32)
    coulomb_coef = coulomb_coef.at[first * ntask + second, third * ntask + fourth].add(2.0 * live)
    coulomb_coef = coulomb_coef.at[third * ntask + fourth, first * ntask + second].add(2.0 * live)
    exchange_coef = jnp.zeros((npairs, npairs), jnp.float32)
    exchange_coef = exchange_coef.at[first * ntask + third, second * ntask + fourth].add(-0.5 * live)
    exchange_coef = exchange_coef.at[first * ntask + fourth, second * ntask + third].add(-0.5 * live)
    exchange_coef = exchange_coef.at[second * ntask + third, first * ntask + fourth].add(-0.5 * live)
    exchange_coef = exchange_coef.at[second * ntask + fourth, first * ntask + third].add(-0.5 * live)
    coulomb_sum = jnp.dot(coulomb_coef, pair_diag.reshape(npairs, points), precision=lax.Precision.HIGHEST)
    coulomb_pot = jnp.dot(coulomb_sum, core, precision=lax.Precision.HIGHEST)
    exchange_sum = jnp.dot(exchange_coef, pairwise.reshape(npairs, points * points), precision=lax.Precision.HIGHEST)
    exchange_sum = exchange_sum.reshape(npairs, points, points)
    identity = jnp.eye(points, dtype=jnp.float32)
    core_matrix = core[None] * exchange_sum + identity[None] * coulomb_pot[:, :, None]
    core_matrix = rounded(core_matrix).reshape(ntask, ntask, points, points)
    right_half = rounded(jnp.einsum("xypq,yqj->xypj", core_matrix, coef))
    return rounded(jnp.einsum("xpi,xypj->xyij", coef, right_half))


def reference(density, factors, core, task_blocks, quartets, quartet_count):
    quads_all = quartets.reshape(N_ROW * N_BULK, Q_DEV, 4)

    def device(fock, inputs):
        blocks, quads, count = inputs
        pieces = device_piece(density, factors, core, blocks, quads, count)
        fock = fock.at[blocks[:, None], blocks[None, :]].add(pieces)
        return fock, None

    fock, _ = lax.scan(device, jnp.zeros(density.shape, jnp.float32), (task_blocks, quads_all, quartet_count))
    return fock
```

```python
import jax
import jax.numpy as jnp
from jax import lax
from jax.experimental import pallas as pl
from jax.experimental.pallas import tpu as pltpu
from jax.sharding import PartitionSpec as P

T = 12
NP = 144
R = 384
BS = 128
CAPE = 512


def entries_kernel(quads, count, lst, start, nxt):
    live = count[0]

    def zero(i, c):
        start[i] = 0
        return c

    lax.fori_loop(0, NP + 1, zero, 0)

    def quad(i):
        return quads[4 * i], quads[4 * i + 1], quads[4 * i + 2], quads[4 * i + 3]

    def add(t):
        start[t + 1] = start[t + 1] + 1

    def tally(i, c):
        a, b, d, e = quad(i)
        add(a * T + d)
        add(a * T + e)
        add(b * T + d)
        add(b * T + e)
        return c

    lax.fori_loop(0, live, tally, 0)

    def running(i, total):
        total = total + start[i + 1]
        start[i + 1] = total
        nxt[i + 1] = total
        return total

    nxt[0] = 0
    lax.fori_loop(0, NP, running, 0)

    def fill(i, c):
        lst[i] = NP
        return c

    lax.fori_loop(0, lst.shape[0], fill, 0)

    def put(t, s):
        at = nxt[t]
        lst[at] = s
        nxt[t] = at + 1

    def place(i, c):
        a, b, d, e = quad(i)
        put(a * T + d, b * T + e)
        put(a * T + e, b * T + d)
        put(b * T + d, a * T + e)
        put(b * T + e, a * T + d)
        return c

    lax.fori_loop(0, live, place, 0)


def entries(quads, count):
    smem = pl.BlockSpec(memory_space=pltpu.SMEM)
    return pl.pallas_call(
        entries_kernel,
        out_shape=[
            jax.ShapeDtypeStruct((CAPE + 128,), jnp.int32),
            jax.ShapeDtypeStruct((256,), jnp.int32),
        ],
        in_specs=[smem, smem],
        out_specs=[smem, smem],
        scratch_shapes=[pltpu.SMEM((256,), jnp.int32)],
        cost_estimate=pl.CostEstimate(flops=10000, bytes_accessed=10000, transcendentals=0),
        name="sort_entries",
    )(quads.reshape(-1), count)


def compute_kernel(ids, in_slot, out_slot, lst, start, core, coul, recv, factors, outbound,
                   dens, fac, fact, half, pieces, pdt, corem, pot, acc, in_sem, fac_sem, out_sem):
    for x in range(T):
        pltpu.make_async_copy(factors.at[ids[x]], fac.at[x], fac_sem).start()
    for x in range(T):
        def fetch(y, c, x=x):
            pltpu.make_async_copy(recv.at[in_slot[x * T + y]], dens.at[x * T + y], in_sem.at[x]).start()
            return c
        lax.fori_loop(0, T, fetch, 0)
    corem[...] = core[...] * -0.5
    half[NP] = jnp.zeros((R, BS), jnp.bfloat16)
    pdt[...] = jnp.zeros_like(pdt)
    pltpu.make_async_copy(factors.at[pl.ds(0, T)], fac, fac_sem).wait()
    for x in range(T):
        fact[x] = fac[x].T

    rowk = lax.broadcasted_iota(jnp.int32, (2 * BS, 256), 0) // BS
    cols = lax.broadcasted_iota(jnp.int32, (2 * BS, 256), 1)
    delta = cols - rowk

    def halves(x, c):
        pltpu.make_async_copy(recv.at[pl.ds(0, T)], dens.at[pl.ds(0, T)], in_sem.at[x]).wait()
        fx = fac[x]
        for yp in range(T // 2):
            s = x * T + 2 * yp
            d2 = jnp.concatenate([dens[s], dens[s + 1]], axis=1)
            h2 = jnp.dot(fx, d2, preferred_element_type=jnp.float32).astype(jnp.bfloat16)
            half[s] = h2[:, :BS]
            half[s + 1] = h2[:, BS:]
            f2 = jnp.concatenate([fac[2 * yp], fac[2 * yp + 1]], axis=1)
            prod = (h2.astype(jnp.float32) * f2.astype(jnp.float32)).astype(jnp.bfloat16)
            spread = (delta == s).astype(jnp.bfloat16)
            pdt[...] += jnp.dot(prod, spread, preferred_element_type=jnp.float32)
        return c

    lax.fori_loop(0, T, halves, 0)
    pair_diag = pdt[...].T
    total = jnp.dot(coul[...], pair_diag, precision=lax.Precision.HIGHEST, preferred_element_type=jnp.float32)
    pot[...] = jnp.dot(total, core[...], precision=lax.Precision.HIGHEST, preferred_element_type=jnp.float32).reshape(NP, 1, R)
    eye = lax.broadcasted_iota(jnp.int32, (BS, BS), 0) == lax.broadcasted_iota(jnp.int32, (BS, BS), 1)

    def target(t, c):
        x = t // T
        y = t % T
        lo = start[t]
        n = (start[t + 1] - lo)

        def pair(k):
            s1 = lst[lo + 2 * k]
            s2 = jnp.where(2 * k + 1 < n, lst[lo + 2 * k + 1], NP)
            y1 = lax.rem(s1, T)
            y2 = lax.rem(s2, T)
            h = jnp.concatenate([half[s1], half[s2]], axis=1)
            w = jnp.concatenate([fact[y1], fact[y2]], axis=0)
            return jnp.dot(h, w, preferred_element_type=jnp.float32)

        acc[...] = jnp.zeros_like(acc)

        def more(k, c):
            acc[...] += pair(k)
            return c

        lax.fori_loop(0, (n + 1) // 2, more, 0)
        row = pot[t]
        cm = corem[...] * acc[...]
        parts = []
        for k in range(3):
            line = cm[k * BS:(k + 1) * BS]
            blk = line[:, k * BS:(k + 1) * BS] + jnp.where(eye, row[:, k * BS:(k + 1) * BS], 0.0)
            cols3 = [line[:, j * BS:(j + 1) * BS] for j in range(3)]
            cols3[k] = blk
            parts.append(jnp.concatenate(cols3, axis=1))
        cm = jnp.concatenate(parts, axis=0).astype(jnp.bfloat16)
        rh = jnp.dot(cm, fac[y], preferred_element_type=jnp.float32).astype(jnp.bfloat16)
        pieces[t] = jnp.dot(fact[x], rh, preferred_element_type=jnp.float32).astype(jnp.bfloat16)
        pltpu.make_async_copy(pieces.at[t], outbound.at[out_slot[t]], out_sem).start()
        return c

    lax.fori_loop(0, NP, target, 0)
    pltpu.make_async_copy(pieces, outbound.at[pl.ds(0, NP)], out_sem).wait()


def compute(ids, in_slot, out_slot, lst, start, core, coul, recv, factors, nslots, kernel=compute_kernel):
    smem = pl.BlockSpec(memory_space=pltpu.SMEM)
    vmem = pl.BlockSpec(memory_space=pltpu.VMEM)
    hbm = pl.BlockSpec(memory_space=pl.ANY)
    return pl.pallas_call(
        kernel,
        out_shape=jax.ShapeDtypeStruct((nslots, BS, BS), jnp.bfloat16),
        in_specs=[smem] * 5 + [vmem] * 2 + [hbm] * 2,
        out_specs=hbm,
        scratch_shapes=[
            pltpu.VMEM((NP, BS, BS), jnp.bfloat16),
            pltpu.VMEM((T, R, BS), jnp.bfloat16),
            pltpu.VMEM((T, BS, R), jnp.bfloat16),
            pltpu.VMEM((NP + 1, R, BS), jnp.bfloat16),
            pltpu.VMEM((NP, BS, BS), jnp.bfloat16),
            pltpu.VMEM((R, 256), jnp.float32),
            pltpu.VMEM((R, R), jnp.float32),
            pltpu.VMEM((NP, 1, R), jnp.float32),
            pltpu.VMEM((R, R), jnp.float32),
            pltpu.SemaphoreType.DMA((T,)),
            pltpu.SemaphoreType.DMA,
            pltpu.SemaphoreType.DMA,
        ],
        compiler_params=pltpu.CompilerParams(vmem_limit_bytes=50 * 2**20),
        cost_estimate=pl.CostEstimate(flops=25 * 10**9, bytes_accessed=12 * 10**6, transcendentals=0),
        name="fock_pieces",
    )(ids, in_slot, out_slot, lst, start, core, coul, recv, factors)


def coulomb_table(quads, count):
    live = (jnp.arange(128, dtype=jnp.int32) < count).astype(jnp.float32)
    p = quads[:, 0] * T + quads[:, 1]
    q = quads[:, 2] * T + quads[:, 3]
    tg = jnp.concatenate([p, q])
    sr = jnp.concatenate([q, p])
    ht = (tg[:, None] == jnp.arange(NP)[None]).astype(jnp.bfloat16)
    hs = jnp.where(sr[:, None] == jnp.arange(256)[None], jnp.concatenate([live, live])[:, None] * 2.0, 0.0).astype(jnp.bfloat16)
    return lax.dot_general(ht, hs, (((0,), (0,)), ((), ())), preferred_element_type=jnp.float32)


def column_of(ids, d, bulk):
    group = bulk // 8
    local = jnp.int32(-1)
    for j in range(3):
        block = ids[d * T + group * 3 + j]
        local = jnp.where(block // 3 == bulk, block % 3, local)
    return local


def pack_kernel(place, ids, density, out, sem):
    row = place[0]
    bulk = place[1]

    def copy(d, j, col):
        r = ids[d * T + row * 3 + j] - row * 24
        return pltpu.make_async_copy(density.at[r, col], out.at[d * 3 + j], sem)

    def send(d, n):
        col = column_of(ids, d, bulk)

        @pl.when(col >= 0)
        def _():
            for j in range(3):
                copy(d, j, col).start()

        return n + (col >= 0).astype(jnp.int32)

    n = lax.fori_loop(0, 128, send, 0)

    def drain(i, c):
        pltpu.make_async_copy(out.at[pl.ds(0, 3)], out.at[pl.ds(0, 3)], sem).wait()
        return c

    lax.fori_loop(0, n, drain, 0)


def pack(place, ids, density):
    smem = pl.BlockSpec(memory_space=pltpu.SMEM)
    hbm = pl.BlockSpec(memory_space=pl.ANY)
    return pl.pallas_call(
        pack_kernel,
        out_shape=jax.ShapeDtypeStruct((384, BS, BS), jnp.bfloat16),
        in_specs=[smem, smem, hbm],
        out_specs=hbm,
        scratch_shapes=[pltpu.SemaphoreType.DMA],
        name="pack_density",
    )(place, ids, density)


def gather_kernel(place, ids, inbound, fock, buf, sems):
    row = place[0]
    bulk = place[1]

    def fetch(d, c):
        @pl.when(column_of(ids, d, bulk) >= 0)
        def _():
            pltpu.make_async_copy(inbound.at[pl.ds(d * 3, 3)], buf.at[pl.ds(d * 3, 3)], sems.at[d]).start()

        return c

    lax.fori_loop(0, 128, fetch, 0)
    fock[...] = jnp.zeros_like(fock)

    def add(d, c):
        col = column_of(ids, d, bulk)

        @pl.when(col >= 0)
        def _():
            pltpu.make_async_copy(inbound.at[pl.ds(d * 3, 3)], buf.at[pl.ds(d * 3, 3)], sems.at[d]).wait()
            for j in range(3):
                r = ids[d * T + row * 3 + j] - row * 24
                fock[r, col] += buf[d * 3 + j].astype(jnp.float32)

        return c

    lax.fori_loop(0, 128, add, 0)


def gather(place, ids, inbound):
    smem = pl.BlockSpec(memory_space=pltpu.SMEM)
    vmem = pl.BlockSpec(memory_space=pltpu.VMEM)
    hbm = pl.BlockSpec(memory_space=pl.ANY)
    return pl.pallas_call(
        gather_kernel,
        out_shape=jax.ShapeDtypeStruct((24, 3, BS, BS), jnp.float32),
        in_specs=[smem, smem, hbm],
        out_specs=vmem,
        scratch_shapes=[pltpu.VMEM((384, BS, BS), jnp.bfloat16), pltpu.SemaphoreType.DMA((128,))],
        compiler_params=pltpu.CompilerParams(vmem_limit_bytes=40 * 2**20),
        name="add_pieces",
    )(place, ids, inbound)


def shards(density, factors, core, task_blocks, quartets, quartet_count):
    axes = ("row", "bulk")
    mine = task_blocks[0]
    place = jnp.stack([lax.axis_index("row"), lax.axis_index("bulk")]).astype(jnp.int32)
    ids = lax.all_to_all(
        jnp.broadcast_to(mine[None], (128, T)), axes, split_axis=0, concat_axis=0, tiled=True
    ).reshape(-1)
    sent = pack(place, ids, density)
    recv = lax.all_to_all(sent, axes, split_axis=0, concat_axis=0, tiled=True)
    lst, start = entries(quartets, quartet_count)
    coul = coulomb_table(quartets, quartet_count[0])
    owner = mine[:, None] // 24 * 32 + mine[None, :] // 3
    slot = (owner * 3 + (jnp.arange(T) % 3)[:, None]).reshape(-1).astype(jnp.int32)
    outbound = compute(mine, slot, slot, lst, start, core, coul, recv, factors, 384)
    inbound = lax.all_to_all(outbound, axes, split_axis=0, concat_axis=0, tiled=True)
    return gather(place, ids, inbound)


def solution(mesh):
    return jax.shard_map(
        shards,
        mesh=mesh,
        in_specs=(
            P("row", "bulk", None, None),
            P(),
            P(),
            P(("row", "bulk"), None),
            P(("row", "bulk"), None),
            P(("row", "bulk")),
        ),
        out_specs=P("row", "bulk", None, None),
        check_vma=False,
    )
```

```python
import functools

import jax
import jax.numpy as jnp
from jax import lax
from jax.experimental import pallas as pl
from jax.experimental.pallas import tpu as pltpu
from jax.sharding import PartitionSpec as P

T = 12
NP = 144
R = 384
BS = 128
CAPE = 512
G = 4
LEVELS = 4


def entries_kernel(quads, count, lst, start, order, nxt):
    live = count[0]

    def zero(i, c):
        start[i] = 0
        return c

    lax.fori_loop(0, NP + 1, zero, 0)

    def quad(i):
        return quads[4 * i], quads[4 * i + 1], quads[4 * i + 2], quads[4 * i + 3]

    def add(t):
        start[t + 1] = start[t + 1] + 1

    def tally(i, c):
        a, b, d, e = quad(i)
        add(a * T + d)
        add(a * T + e)
        add(b * T + d)
        add(b * T + e)
        return c

    lax.fori_loop(0, live, tally, 0)

    def running(i, total):
        total = total + start[i + 1]
        start[i + 1] = total
        nxt[i + 1] = total
        return total

    nxt[0] = 0
    lax.fori_loop(0, NP, running, 0)

    def fill(i, c):
        lst[i] = NP
        return c

    lax.fori_loop(0, lst.shape[0], fill, 0)

    def put(t, s):
        at = nxt[t]
        lst[at] = s
        nxt[t] = at + 1

    def place(i, c):
        a, b, d, e = quad(i)
        put(a * T + d, b * T + e)
        put(a * T + e, b * T + d)
        put(b * T + d, a * T + e)
        put(b * T + e, a * T + d)
        return c

    lax.fori_loop(0, live, place, 0)

    def level(t):
        return jnp.minimum((start[t + 1] - start[t] + 1) // 2, LEVELS + 1)

    for k in range(LEVELS + 3):
        nxt[k] = 0

    def classes(t, c):
        k = LEVELS + 1 - level(t)
        nxt[k + 1] = nxt[k + 1] + 1
        return c

    lax.fori_loop(0, NP, classes, 0)
    for k in range(LEVELS + 2):
        nxt[k + 1] = nxt[k + 1] + nxt[k]

    def pad(i, c):
        order[i] = NP
        return c

    lax.fori_loop(0, order.shape[0], pad, 0)

    def rank(t, c):
        k = LEVELS + 1 - level(t)
        at = nxt[k]
        order[2 * G + at] = t
        nxt[k] = at + 1
        return c

    lax.fori_loop(0, NP, rank, 0)


def entries(quads, count):
    smem = pl.BlockSpec(memory_space=pltpu.SMEM)
    return pl.pallas_call(
        entries_kernel,
        out_shape=[
            jax.ShapeDtypeStruct((CAPE + 128,), jnp.int32),
            jax.ShapeDtypeStruct((256,), jnp.int32),
            jax.ShapeDtypeStruct((256,), jnp.int32),
        ],
        in_specs=[smem, smem],
        out_specs=[smem, smem, smem],
        scratch_shapes=[pltpu.SMEM((256,), jnp.int32)],
        cost_estimate=pl.CostEstimate(flops=10000, bytes_accessed=10000, transcendentals=0),
        name="sort_entries",
    )(quads.reshape(-1), count)


def slot_of(direct, slots, t):
    if direct:
        return t
    x = t // T
    y = lax.rem(t, T)
    return lax.rem(x, 3) * 64 + x // 3 * 16 + y // 3 * 4 + slots[y]


def compute_kernel(direct, ids, slots, lst, start, order, core, coul, recv, factors, outbound,
                   dens, fac, fact, half, pieces, pdt, corem, pot, acc, cms, rhs, in_sem, fac_sem, out_sem):
    for x in range(T):
        pltpu.make_async_copy(factors.at[ids[x]], fac.at[x], fac_sem).start()
    for x in range(T):
        def fetch(y, c, x=x):
            pltpu.make_async_copy(recv.at[slot_of(direct, slots, x * T + y)], dens.at[x * T + y], in_sem.at[x]).start()
            return c
        lax.fori_loop(0, T, fetch, 0)
    corem[...] = core[...] * -0.5
    half[NP] = jnp.zeros((R, BS), jnp.bfloat16)
    pdt[...] = jnp.zeros_like(pdt)
    pltpu.make_async_copy(factors.at[pl.ds(0, T)], fac, fac_sem).wait()
    for x in range(T):
        fact[x] = fac[x].T

    rowk = lax.broadcasted_iota(jnp.int32, (2 * BS, 256), 0) // BS
    cols = lax.broadcasted_iota(jnp.int32, (2 * BS, 256), 1)
    delta = cols - rowk

    def halves(x, c):
        pltpu.make_async_copy(recv.at[pl.ds(0, T)], dens.at[pl.ds(0, T)], in_sem.at[x]).wait()
        fx = fac[x]
        for yp in range(T // 2):
            s = x * T + 2 * yp
            d2 = jnp.concatenate([dens[s], dens[s + 1]], axis=1)
            h2 = jnp.dot(fx, d2, preferred_element_type=jnp.float32).astype(jnp.bfloat16)
            half[s] = h2[:, :BS]
            half[s + 1] = h2[:, BS:]
            f2 = jnp.concatenate([fac[2 * yp], fac[2 * yp + 1]], axis=1)
            prod = (h2.astype(jnp.float32) * f2.astype(jnp.float32)).astype(jnp.bfloat16)
            spread = (delta == s).astype(jnp.bfloat16)
            pdt[...] += jnp.dot(prod, spread, preferred_element_type=jnp.float32)
        return c

    lax.fori_loop(0, T, halves, 0)
    pair_diag = pdt[...].T
    total = jnp.dot(coul[...], pair_diag, precision=lax.Precision.HIGHEST, preferred_element_type=jnp.float32)
    pot[...] = jnp.dot(total, core[...], precision=lax.Precision.HIGHEST, preferred_element_type=jnp.float32).reshape(NP, 1, R)
    eye = lax.broadcasted_iota(jnp.int32, (BS, BS), 0) == lax.broadcasted_iota(jnp.int32, (BS, BS), 1)


    def gather_pairs(lo, n, first, pairs):
        hs, ws = [], []
        for k in range(2 * pairs):
            e = first + k
            s = jnp.where(e < n, lst[lo + e], NP)
            hs.append(half[s])
            ws.append(fact[lax.rem(s, T)])
        return jnp.dot(
            jnp.concatenate(hs, axis=1), jnp.concatenate(ws, axis=0), preferred_element_type=jnp.float32
        )

    def with_diag(cm, row):
        parts = []
        for k in range(3):
            line = cm[k * BS:(k + 1) * BS]
            cols3 = [line[:, j * BS:(j + 1) * BS] for j in range(3)]
            cols3[k] = cols3[k] + jnp.where(eye, row[:, k * BS:(k + 1) * BS], 0.0)
            parts.append(jnp.concatenate(cols3, axis=1))
        return jnp.concatenate(parts, axis=0).astype(jnp.bfloat16)

    def step(i, c):
        now = lax.rem(i, 2)
        before = 1 - now
        tg = [order[2 * G + i * G + q] for q in range(G)]
        t1 = [order[G + i * G + q] for q in range(G)]
        t2 = [order[i * G + q] for q in range(G)]

        def exchange(t, q, pairs, extra):
            lo = start[t]
            n = start[t + 1] - lo
            if extra:
                acc[...] = jnp.zeros_like(acc)

                def more(k, c):
                    acc[...] += gather_pairs(lo, n, 2 * k, 1)
                    return c

                lax.fori_loop(pairs, (n + 1) // 2, more, 0)
            if pairs:
                es = gather_pairs(lo, n, 0, pairs)
                if extra:
                    es = es + acc[...]
                cm = corem[...] * es
            else:
                cm = jnp.zeros((R, R), jnp.float32)
            cms[now, q] = with_diag(cm, pot[t])

        def late():
            for q in range(G):
                x2 = jnp.minimum(t2[q], NP - 1) // T
                pieces[t2[q]] = jnp.dot(
                    fact[x2], rhs[now, q], preferred_element_type=jnp.float32
                ).astype(jnp.bfloat16)
            for q in range(G):
                y1 = lax.rem(t1[q], T)
                rhs[before, q] = jnp.dot(
                    cms[before, q], fac[y1], preferred_element_type=jnp.float32
                ).astype(jnp.bfloat16)

        def branch(pairs, extra):
            def run():
                late()
                for q in range(G):
                    exchange(tg[q], q, pairs, extra)
            return run

        top = start[tg[0] + 1] - start[tg[0]]
        top = jnp.where(i < NP // G, (top + 1) // 2, -1)
        lax.switch(
            jnp.minimum(top, LEVELS + 1) + 1,
            [late] + [branch(k, False) for k in range(LEVELS + 1)] + [branch(LEVELS, True)],
        )
        for q in range(G):
            @pl.when(i >= 2)
            def _(q=q):
                pltpu.make_async_copy(pieces.at[t2[q]], outbound.at[slot_of(direct, slots, t2[q])], out_sem).start()
        return c

    lax.fori_loop(0, NP // G + 2, step, 0)
    pltpu.make_async_copy(pieces.at[pl.ds(0, NP)], outbound.at[pl.ds(0, NP)], out_sem).wait()


def compute(ids, slots, lst, start, order, core, coul, recv, factors, nslots, direct=False):
    smem = pl.BlockSpec(memory_space=pltpu.SMEM)
    vmem = pl.BlockSpec(memory_space=pltpu.VMEM)
    hbm = pl.BlockSpec(memory_space=pl.ANY)
    return pl.pallas_call(
        functools.partial(compute_kernel, direct),
        out_shape=jax.ShapeDtypeStruct((nslots, BS, BS), jnp.bfloat16),
        in_specs=[smem] * 5 + [vmem] * 2 + [hbm] * 2,
        out_specs=hbm,
        scratch_shapes=[
            pltpu.VMEM((NP, BS, BS), jnp.bfloat16),
            pltpu.VMEM((T, R, BS), jnp.bfloat16),
            pltpu.VMEM((T, BS, R), jnp.bfloat16),
            pltpu.VMEM((NP + 1, R, BS), jnp.bfloat16),
            pltpu.VMEM((NP + 1, BS, BS), jnp.bfloat16),
            pltpu.VMEM((R, 256), jnp.float32),
            pltpu.VMEM((R, R), jnp.float32),
            pltpu.VMEM((NP, 1, R), jnp.float32),
            pltpu.VMEM((R, R), jnp.float32),
            pltpu.VMEM((2, G, R, R), jnp.bfloat16),
            pltpu.VMEM((2, G, R, BS), jnp.bfloat16),
            pltpu.SemaphoreType.DMA((T,)),
            pltpu.SemaphoreType.DMA,
            pltpu.SemaphoreType.DMA,
        ],
        compiler_params=pltpu.CompilerParams(vmem_limit_bytes=50 * 2**20),
        cost_estimate=pl.CostEstimate(flops=25 * 10**9, bytes_accessed=12 * 10**6, transcendentals=0),
        name="fock_pieces_direct" if direct else "fock_pieces",
    )(ids, slots, lst, start, order, core, coul, recv, factors)


def coulomb_table(quads, count):
    live = (jnp.arange(128, dtype=jnp.int32) < count).astype(jnp.float32)
    p = quads[:, 0] * T + quads[:, 1]
    q = quads[:, 2] * T + quads[:, 3]
    tg = jnp.concatenate([p, q])
    sr = jnp.concatenate([q, p])
    ht = (tg[:, None] == jnp.arange(NP)[None]).astype(jnp.bfloat16)
    hs = jnp.where(sr[:, None] == jnp.arange(256)[None], jnp.concatenate([live, live])[:, None] * 2.0, 0.0).astype(jnp.bfloat16)
    return lax.dot_general(ht, hs, (((0,), (0,)), ((), ())), preferred_element_type=jnp.float32)


CAP = 10
RELAY = 144
MESH = pl.DeviceIdType.MESH
ORDERS = ((2, 1, 0), (1, 0, 2), (0, 2, 1))


def line_of(u):
    chip = [(v * 43) >> 8 for v in u]
    col = [v - 6 * q for v, q in zip(u, chip)]
    e01 = chip[0] == chip[1]
    e02 = chip[0] == chip[2]
    e12 = chip[1] == chip[2]
    twice = e01 | e02 | e12
    over1 = e01
    over2 = e02 | e12
    where2 = jnp.where(e12, chip[1], chip[0])
    over_col = jnp.where(e01, col[1], col[2])
    third = jnp.where(e01, chip[2], jnp.where(e02, chip[1], chip[0]))
    rel = (third - where2) & 3
    return chip, col, twice, over1, over2, where2, over_col, rel


def route_kernel(place, ids, tab, lists, idt, plus_s, minus_s, rankp_s, rankm_s):
    z, y, x, c = place[0], place[1], place[2], place[3]
    idt[...] = ids[...].astype(jnp.float32).T.astype(jnp.int32)
    lane = lax.broadcasted_iota(jnp.int32, (1, 128), 1)
    rows8 = lax.broadcasted_iota(jnp.int32, (8, 128), 0)
    lanes8 = lax.broadcasted_iota(jnp.int32, (8, 128), 1)
    f32 = jnp.float32
    below = (
        lax.broadcasted_iota(jnp.int32, (128, 128), 0) < lax.broadcasted_iota(jnp.int32, (128, 128), 1)
    ).astype(f32).astype(jnp.bfloat16)

    def prefix(m):
        return jnp.dot(m.astype(jnp.bfloat16), below, preferred_element_type=f32)

    lines = []
    fp, fm, fl = [], [], []
    for g in range(4):
        u = [idt[3 * g + j:3 * g + j + 1, :] - 24 * g for j in range(3)]
        ln = line_of(u)
        lines.append(ln)
        chip, col, twice, over1, over2, where2, over_col, rel = ln
        kind = jnp.where(twice, rel, 0)
        at = jnp.broadcast_to(where2, (8, 128)) == rows8 // 2
        here = at & ((lanes8 & 1) == (rows8 & 1))
        kind8 = jnp.broadcast_to(kind, (8, 128))
        fp.append(jnp.where(here & (kind8 == 3), 1.0, 0.0))
        fm.append(jnp.where(here & (kind8 == 1), 1.0, 0.0))
        fl.append(jnp.where(here & (kind8 == 2), 1.0, 0.0))
    fp = jnp.concatenate(fp, axis=0)
    fm = jnp.concatenate(fm, axis=0)
    fl = jnp.concatenate(fl, axis=0)
    np_ = jnp.sum(fp, axis=1, keepdims=True)
    nm_ = jnp.sum(fm, axis=1, keepdims=True)
    nl_ = jnp.sum(fl, axis=1, keepdims=True)
    give = jnp.clip(jnp.floor((nl_ + nm_ - np_ + 1.0) * 0.5), 0.0, nl_)
    first = fl * jnp.where(prefix(fl) < give, 1.0, 0.0)
    plus = fp + first
    minus = fm + fl - first
    plus_s[...] = plus
    minus_s[...] = minus
    rankp_s[...] = prefix(plus)
    rankm_s[...] = prefix(minus)
    most = jnp.max(jnp.maximum(jnp.sum(plus, axis=1, keepdims=True), jnp.sum(minus, axis=1, keepdims=True)), axis=0, keepdims=True)

    me = ((z * 4 + y) * 4 + x) * 2 + c
    own = jnp.zeros((1, 128), jnp.int32)
    for g in range(4):
        chip, col, twice, over1, over2, where2, over_col, rel = lines[g]
        goes = jnp.sum(plus[8 * g:8 * g + 8], axis=0, keepdims=True) > 0.5
        to = (where2 + jnp.where(goes, 1, 3)) & 3
        slots = [chip[0], jnp.where(over1, to, chip[1]), jnp.where(over2, to, chip[2])]
        for j in range(3):
            mine = jnp.sum(jnp.where(lane == me, slots[j], 0).astype(f32), axis=1, keepdims=True)
            own = own + jnp.where(lane == 3 * g + j, mine.astype(jnp.int32), 0)
    own = own + jnp.where(lane == 127, (most > CAP + 0.5).astype(jnp.int32), 0)

    u = [idt[pl.ds(3 * y + j, 1), :] - 24 * y for j in range(3)]
    chip, col, twice, over1, over2, where2, over_col, rel = line_of(u)
    rk = [idt[pl.ds(3 * z + k, 1), :] - 24 * z for k in range(3)]
    line_row = y * 8 + x * 2 + c
    left_row = y * 8 + ((x + 3) & 3) * 2 + c
    right_row = y * 8 + ((x + 1) & 3) * 2 + c

    def pool_col(v):
        core = jnp.where(v >= 3, 1, 0)
        return jnp.where(core == c, 0, 72) + v - 3 * core

    main = jnp.full((1, 128), -1, jnp.int32)
    for j, over in enumerate((chip[0] < 0, over1, over2)):
        main = jnp.where((chip[j] == x) & jnp.logical_not(over), pool_col(col[j]), main)
    from_left = plus_s[pl.ds(left_row, 1), :] > 0.5
    rank_left = rankp_s[pl.ds(left_row, 1), :].astype(jnp.int32)
    from_right = minus_s[pl.ds(right_row, 1), :] > 0.5
    rank_right = rankm_s[pl.ds(right_row, 1), :].astype(jnp.int32)
    for k in range(3):
        idx = jnp.where(main >= 0, main + rk[k] * 3, -1)
        idx = jnp.where(from_left, RELAY + rank_left, idx)
        idx = jnp.where(from_right, RELAY + CAP + rank_right, idx)
        tab[k:k + 1, :] = idx
    tab[3:7, :] = jnp.zeros((4, 128), jnp.int32)
    tab[7:8, :] = own

    j16 = lax.broadcasted_iota(jnp.int32, (16, 128), 0)
    l16 = lax.broadcasted_iota(jnp.int32, (16, 128), 1)
    out = jnp.zeros((16, 128), jnp.int32)

    def listed(flag, rank, value):
        sel = jnp.broadcast_to(flag, (16, 128)) & (jnp.broadcast_to(rank, (16, 128)) == j16)
        got = jnp.sum(jnp.where(sel, jnp.broadcast_to(value, (16, 128)) + 1, 0).astype(f32), axis=1, keepdims=True)
        return got.astype(jnp.int32) - 1

    my_plus = plus_s[pl.ds(line_row, 1), :] > 0.5
    my_rankp = rankp_s[pl.ds(line_row, 1), :].astype(jnp.int32)
    my_minus = minus_s[pl.ds(line_row, 1), :] > 0.5
    my_rankm = rankm_s[pl.ds(line_row, 1), :].astype(jnp.int32)
    for k in range(3):
        value = pool_col(over_col) + rk[k] * 3
        out = jnp.where(l16 == k, listed(my_plus, my_rankp, value), out)
        out = jnp.where(l16 == 3 + k, listed(my_minus, my_rankm, value), out)
    out = jnp.where(l16 == 6, listed(from_left, rank_left, lane), out)
    out = jnp.where(l16 == 7, listed(from_right, rank_right, lane), out)
    lists[...] = out


def route(place, ids):
    smem = pl.BlockSpec(memory_space=pltpu.SMEM)
    vmem = pl.BlockSpec(memory_space=pltpu.VMEM)
    return pl.pallas_call(
        route_kernel,
        out_shape=[jax.ShapeDtypeStruct((8, 128), jnp.int32), jax.ShapeDtypeStruct((16, 128), jnp.int32)],
        in_specs=[smem, vmem],
        out_specs=[vmem, vmem],
        scratch_shapes=[pltpu.VMEM((128, 128), jnp.int32)] + [pltpu.VMEM((32, 128), jnp.float32)] * 4,
        name="route_tasks",
    )(place, ids)


def here():
    z = lax.axis_index("row")
    b = lax.axis_index("bulk")
    return b // 2 % 4, b // 8, z, b % 2


def device(x, y, z, c):
    return (z, y * 8 + x * 2 + c)


def moved(at, axis, by):
    pos = list(at[:3])
    pos[axis] = lax.rem(pos[axis] + by, 4)
    return device(*pos, at[3])


def greet(at):
    barrier = pltpu.get_barrier_semaphore()
    for axis in range(3):
        for by in (1, 2, 3):
            pl.semaphore_signal(barrier, inc=1, device_id=moved(at, axis, by), device_id_type=MESH)
    pl.semaphore_wait(barrier, 9)


def part(ref, axis, index):
    if axis == 2:
        return ref.at[index]
    if axis == 1:
        return ref.at[:, index]
    return ref.at[:, :, index]


def phase_copies(at, k, step, src, dst, send, recv, local):
    axis = ORDERS[k][step]
    own = at[axis]
    copies = [pltpu.make_async_copy(part(src, axis, own), part(dst, axis, own), local.at[k, step])]
    for by in (1, 2, 3):
        to = lax.rem(own + by, 4)
        copies.append(
            pltpu.make_async_remote_copy(
                part(src, axis, to), part(dst, axis, own),
                send.at[k, step, by - 1], recv.at[k, step, by - 1],
                device_id=moved(at, axis, by), device_id_type=MESH,
            )
        )
    return copies


def start_all(copies):
    for copy in copies:
        copy.start()


def wait_all(copies):
    for copy in copies:
        copy.wait()


def fetch_kernel(tab, lists, density, sibling, out, pool, r0, r1, r2, rs, a, b, d,
                 load, relay_send, relay_recv, send, recv, local):
    at = here()
    c = at[3]
    mine = pltpu.make_async_copy(density, pool.at[pl.ds(0, 72)], load.at[0])
    other = pltpu.make_async_copy(sibling, pool.at[pl.ds(72, 72)], load.at[1])
    mine.start()
    other.start()
    greet(at)
    mine.wait()
    other.wait()
    relayed = (r0, r1, r2)
    relays = []
    for k in range(3):
        def fill(j, cc, k=k):
            rs[k, j] = pool[jnp.maximum(lists[j, k], 0)]
            rs[k, CAP + j] = pool[jnp.maximum(lists[j, 3 + k], 0)]
            return cc
        lax.fori_loop(0, CAP, fill, 0)
        pair = [
            pltpu.make_async_remote_copy(
                rs.at[k, pl.ds(CAP * side, CAP)], relayed[k].at[pl.ds(CAP * side, CAP)],
                relay_send.at[k, side], relay_recv.at[k, side],
                device_id=moved(at, 0, 1 if side == 0 else 3), device_id_type=MESH,
            )
            for side in range(2)
        ]
        start_all(pair)
        relays.append(pair)
    steps = []
    for k in range(3):
        wait_all(relays[k])

        def fill(i, cc, k=k):
            index = tab[k, 2 * i + c]
            plain = pool[jnp.clip(index, 0, 143)]
            passed = relayed[k][jnp.maximum(index - RELAY, 0)]
            a[k, i // 16, i // 4 % 4, i % 4] = jnp.where(index >= RELAY, passed, plain)
            return cc

        lax.fori_loop(0, 64, fill, 0)
        copies = phase_copies(at, k, 0, a.at[k], b.at[k], send, recv, local)
        start_all(copies)
        steps.append(copies)
    for step, src, dst in ((1, b, d), (2, d, out)):
        for k in range(3):
            wait_all(steps[k])
            copies = phase_copies(at, k, step, src.at[k], dst.at[k], send, recv, local)
            start_all(copies)
            steps[k] = copies
    for k in range(3):
        wait_all(steps[k])


def fetch_blocks(tab, lists, density, sibling):
    smem = pl.BlockSpec(memory_space=pltpu.SMEM)
    hbm = pl.BlockSpec(memory_space=pl.ANY)
    cube = pltpu.VMEM((3, 4, 4, 4, BS, BS), jnp.bfloat16)
    dma = pltpu.SemaphoreType.DMA
    return pl.pallas_call(
        fetch_kernel,
        out_shape=jax.ShapeDtypeStruct((3, 4, 4, 4, BS, BS), jnp.bfloat16),
        in_specs=[smem, smem, hbm, hbm],
        out_specs=hbm,
        scratch_shapes=[pltpu.VMEM((144, BS, BS), jnp.bfloat16)]
        + [pltpu.VMEM((2 * CAP, BS, BS), jnp.bfloat16)] * 3
        + [pltpu.VMEM((3, 2 * CAP, BS, BS), jnp.bfloat16), cube, cube, cube]
        + [dma((2,)), dma((3, 2)), dma((3, 2)), dma((3, 3, 3)), dma((3, 3, 3)), dma((3, 3))],
        compiler_params=pltpu.CompilerParams(
            collective_id=1, has_side_effects=True, vmem_limit_bytes=50 * 2**20
        ),
        name="fetch_blocks",
    )(tab, lists, density.reshape(72, BS, BS), sibling.reshape(72, BS, BS))


def return_kernel(lists, pieces, out, back, b, d, e0, e1, e2, rs,
                  relay_send, relay_recv, send, recv, local, store):
    at = here()
    greet(at)
    ends = (e0, e1, e2)
    steps = []
    for k in range(3):
        copies = phase_copies(at, k, 0, pieces.at[k], b.at[k], send, recv, local)
        start_all(copies)
        steps.append(copies)
    for k in range(3):
        wait_all(steps[k])
        steps[k] = phase_copies(at, k, 1, b.at[k], d.at[k], send, recv, local)
        start_all(steps[k])
    for k in range(3):
        wait_all(steps[k])
        steps[k] = phase_copies(at, k, 2, d.at[k], ends[k], send, recv, local)
        start_all(steps[k])
    for k in range(3):
        wait_all(steps[k])
        kept = pltpu.make_async_copy(ends[k], out.at[k], store.at[k])
        kept.start()

        def fill(j, cc, k=k):
            for side in range(2):
                t = jnp.maximum(lists[j, 6 + side], 0) // 2
                rs[k, side * CAP + j] = ends[k][t // 16, t // 4 % 4, t % 4]
            return cc

        lax.fori_loop(0, CAP, fill, 0)
        pair = [
            pltpu.make_async_remote_copy(
                rs.at[k, pl.ds(CAP * side, CAP)], back.at[k, pl.ds(CAP * side, CAP)],
                relay_send.at[k, side], relay_recv.at[k, side],
                device_id=moved(at, 0, 3 if side == 0 else 1), device_id_type=MESH,
            )
            for side in range(2)
        ]
        start_all(pair)
        steps[k] = pair + [kept]
    for k in range(3):
        wait_all(steps[k])


def return_pieces(lists, pieces):
    smem = pl.BlockSpec(memory_space=pltpu.SMEM)
    hbm = pl.BlockSpec(memory_space=pl.ANY)
    cube = pltpu.VMEM((3, 4, 4, 4, BS, BS), jnp.bfloat16)
    dma = pltpu.SemaphoreType.DMA
    return pl.pallas_call(
        return_kernel,
        out_shape=[
            jax.ShapeDtypeStruct((3, 4, 4, 4, BS, BS), jnp.bfloat16),
            jax.ShapeDtypeStruct((3, 2 * CAP, BS, BS), jnp.bfloat16),
        ],
        in_specs=[smem, hbm],
        out_specs=[hbm, hbm],
        scratch_shapes=[cube, cube]
        + [pltpu.VMEM((4, 4, 4, BS, BS), jnp.bfloat16)] * 3
        + [pltpu.VMEM((3, 2 * CAP, BS, BS), jnp.bfloat16)]
        + [dma((3, 2)), dma((3, 2)), dma((3, 3, 3)), dma((3, 3, 3)), dma((3, 3)), dma((3,))],
        compiler_params=pltpu.CompilerParams(
            collective_id=2, has_side_effects=True, vmem_limit_bytes=50 * 2**20
        ),
        name="return_pieces",
    )(lists, pieces)


def collect_kernel(place, tab, lists, got, back, own, other, acc):
    c = place[3]
    acc[...] = jnp.zeros_like(acc)
    own[...] = jnp.zeros_like(own)

    def put(index, block):
        @pl.when((index >= 0) & (index < 72))
        def _():
            own[jnp.clip(index, 0, 71)] += block().astype(jnp.float32)

        @pl.when((index >= 72) & (index < 144))
        def _():
            acc[jnp.clip(index - 72, 0, 71)] += block().astype(jnp.float32)

    def add(i, cc):
        for k in range(3):
            put(tab[k, 2 * i + c], lambda: got[k, i])
        return cc

    lax.fori_loop(0, 64, add, 0)

    def add_back(j, cc):
        for k in range(3):
            for side in range(2):
                put(lists[j, 3 * side + k], lambda: back[k, side * CAP + j])
        return cc

    lax.fori_loop(0, CAP, add_back, 0)
    other[...] = acc[...].astype(jnp.bfloat16)


def collect(place, tab, lists, got, back):
    smem = pl.BlockSpec(memory_space=pltpu.SMEM)
    vmem = pl.BlockSpec(memory_space=pltpu.VMEM)
    return pl.pallas_call(
        collect_kernel,
        out_shape=[
            jax.ShapeDtypeStruct((72, BS, BS), jnp.float32),
            jax.ShapeDtypeStruct((72, BS, BS), jnp.bfloat16),
        ],
        in_specs=[smem, smem, smem, vmem, vmem],
        out_specs=[vmem, vmem],
        scratch_shapes=[pltpu.VMEM((72, BS, BS), jnp.float32)],
        compiler_params=pltpu.CompilerParams(vmem_limit_bytes=50 * 2**20),
        name="collect_pieces",
    )(place, tab, lists, got.reshape(3, 64, BS, BS), back)


def swap_cores(value):
    return lax.ppermute(value, "bulk", [(i, i ^ 1) for i in range(32)])


def fast_path(density, factors, core, mine, sibling, tables, place, tab, lists, coul):
    recv = fetch_blocks(tab, lists, density, sibling).reshape(192, BS, BS)
    pieces = compute(mine, tab[7], *tables, core, coul, recv, factors, 192)
    got, back = return_pieces(lists, pieces.reshape(3, 4, 4, 4, BS, BS))
    own, other = collect(place, tab, lists, got, back)
    return (own + swap_cores(other).astype(jnp.float32)).reshape(24, 3, BS, BS)


def column_of(ids, d, bulk):
    group = bulk // 8
    local = jnp.int32(-1)
    for j in range(3):
        block = ids[d * T + group * 3 + j]
        local = jnp.where(block // 3 == bulk, block % 3, local)
    return local


def pack_kernel(place, ids, density, out, sem):
    row = place[0]
    bulk = place[1]

    def copy(d, j, col):
        r = ids[d * T + row * 3 + j] - row * 24
        return pltpu.make_async_copy(density.at[r, col], out.at[d * 3 + j], sem)

    def send(d, n):
        col = column_of(ids, d, bulk)

        @pl.when(col >= 0)
        def _():
            for j in range(3):
                copy(d, j, col).start()

        return n + (col >= 0).astype(jnp.int32)

    n = lax.fori_loop(0, 128, send, 0)

    def drain(i, c):
        pltpu.make_async_copy(out.at[pl.ds(0, 3)], out.at[pl.ds(0, 3)], sem).wait()
        return c

    lax.fori_loop(0, n, drain, 0)


def pack(place, ids, density):
    smem = pl.BlockSpec(memory_space=pltpu.SMEM)
    hbm = pl.BlockSpec(memory_space=pl.ANY)
    return pl.pallas_call(
        pack_kernel,
        out_shape=jax.ShapeDtypeStruct((384, BS, BS), jnp.bfloat16),
        in_specs=[smem, smem, hbm],
        out_specs=hbm,
        scratch_shapes=[pltpu.SemaphoreType.DMA],
        name="pack_density",
    )(place, ids, density)


def gather_kernel(place, ids, inbound, fock, buf, sems):
    row = place[0]
    bulk = place[1]

    def fetch(d, c):
        @pl.when(column_of(ids, d, bulk) >= 0)
        def _():
            pltpu.make_async_copy(inbound.at[pl.ds(d * 3, 3)], buf.at[pl.ds(d * 3, 3)], sems.at[d]).start()

        return c

    lax.fori_loop(0, 128, fetch, 0)
    fock[...] = jnp.zeros_like(fock)

    def add(d, c):
        col = column_of(ids, d, bulk)

        @pl.when(col >= 0)
        def _():
            pltpu.make_async_copy(inbound.at[pl.ds(d * 3, 3)], buf.at[pl.ds(d * 3, 3)], sems.at[d]).wait()
            for j in range(3):
                r = ids[d * T + row * 3 + j] - row * 24
                fock[r, col] += buf[d * 3 + j].astype(jnp.float32)

        return c

    lax.fori_loop(0, 128, add, 0)


def gather(place, ids, inbound):
    smem = pl.BlockSpec(memory_space=pltpu.SMEM)
    vmem = pl.BlockSpec(memory_space=pltpu.VMEM)
    hbm = pl.BlockSpec(memory_space=pl.ANY)
    return pl.pallas_call(
        gather_kernel,
        out_shape=jax.ShapeDtypeStruct((24, 3, BS, BS), jnp.float32),
        in_specs=[smem, smem, hbm],
        out_specs=vmem,
        scratch_shapes=[pltpu.VMEM((384, BS, BS), jnp.bfloat16), pltpu.SemaphoreType.DMA((128,))],
        compiler_params=pltpu.CompilerParams(vmem_limit_bytes=40 * 2**20),
        name="add_pieces",
    )(place, ids, inbound)


def slow_path(density, factors, core, mine, tables, place, ids, coul):
    axes = ("row", "bulk")
    where = jnp.stack([place[0], place[1] * 8 + place[2] * 2 + place[3]])
    ids = ids[:, :T].reshape(-1)
    sent = pack(where, ids, density)
    recv = lax.all_to_all(sent, axes, split_axis=0, concat_axis=0, tiled=True)
    owner = mine[:, None] // 24 * 32 + mine[None, :] // 3
    slot = (owner * 3 + (jnp.arange(T) % 3)[:, None]).reshape(-1)
    pieces = compute(mine, mine, *tables, core, coul, recv[slot], factors, NP, direct=True)
    outbound = jnp.zeros((384, BS, BS), jnp.bfloat16).at[slot].set(pieces)
    inbound = lax.all_to_all(outbound, axes, split_axis=0, concat_axis=0, tiled=True)
    return gather(where, ids, inbound)


def shards(density, factors, core, task_blocks, quartets, quartet_count):
    axes = ("row", "bulk")
    mine = task_blocks[0]
    bulk = lax.axis_index("bulk")
    place = jnp.stack([lax.axis_index("row"), bulk // 8, bulk // 2 % 4, bulk % 2]).astype(jnp.int32)
    ids = lax.all_to_all(
        jnp.broadcast_to(jnp.pad(mine, (0, 116))[None], (128, 128)), axes, split_axis=0, concat_axis=0, tiled=True
    )
    sibling = swap_cores(density)
    tables = entries(quartets, quartet_count)
    coul = coulomb_table(quartets, quartet_count[0])
    tab, lists = route(place, ids)
    return lax.cond(
        tab[7, 127] > 0,
        lambda: slow_path(density, factors, core, mine, tables, place, ids, coul),
        lambda: fast_path(density, factors, core, mine, sibling, tables, place, tab, lists, coul),
    )


def solution(mesh):
    return jax.shard_map(
        shards,
        mesh=mesh,
        in_specs=(
            P("row", "bulk", None, None),
            P(),
            P(),
            P(("row", "bulk"), None),
            P(("row", "bulk"), None),
            P(("row", "bulk")),
        ),
        out_specs=P("row", "bulk", None, None),
        check_vma=False,
    )
```

```python
import functools

import jax
import jax.numpy as jnp
from jax import lax
from jax.experimental import pallas as pl
from jax.experimental.pallas import tpu as pltpu
from jax.sharding import PartitionSpec as P

T = 12
NP = 144
R = 384
BS = 128
CAPE = 512
G = 4
LEVELS = 7
STRIP = 64


def entries_kernel(quads, count, tables, coul):
    f32 = jnp.float32
    live = lax.broadcasted_iota(jnp.int32, (128, 1), 0) < count[0]
    q = quads[...]
    a, b, c, e = (q[:, n:n + 1] for n in range(4))
    lanes = lax.broadcasted_iota(jnp.int32, (128, 256), 1)

    def hot(t):
        return jnp.where((t == lanes) & live, 1.0, 0.0)

    def product(u, v):
        return jnp.dot(u.T.astype(jnp.bfloat16), v.astype(jnp.bfloat16), preferred_element_type=f32)

    bra = hot(a * T + b)
    ket = hot(c * T + e)
    table = 2.0 * (product(bra, ket) + product(ket, bra))
    coul[...] = table[:NP, :NP]

    targets = [a * T + c, a * T + e, b * T + c, b * T + e]
    sources = [b * T + e, b * T + c, a * T + e, a * T + c]
    member = jnp.concatenate([hot(t) for t in targets], axis=0)
    source = jnp.concatenate(sources, axis=0).astype(f32)
    older = lax.broadcasted_iota(jnp.int32, (CAPE, CAPE), 0) > lax.broadcasted_iota(jnp.int32, (CAPE, CAPE), 1)
    rank = jnp.dot(
        jnp.where(older, 1.0, 0.0).astype(jnp.bfloat16), member.astype(jnp.bfloat16), preferred_element_type=f32
    )
    counts = jnp.broadcast_to(jnp.sum(member, axis=0, keepdims=True), (8, 256))
    row = lax.broadcasted_iota(jnp.int32, (256, 256), 0)
    col = lax.broadcasted_iota(jnp.int32, (256, 256), 1)
    start = jnp.dot(
        counts, jnp.where(row < col, 1.0, 0.0), precision=lax.Precision.HIGHEST, preferred_element_type=f32
    )
    used = jnp.sum(member, axis=1, keepdims=True) > 0.5
    place = jnp.sum(member * (rank + start[0:1]), axis=1, keepdims=True)
    place = jnp.where(used, place, -1.0).astype(jnp.int32)
    spots = lax.broadcasted_iota(jnp.int32, (CAPE, CAPE + 128), 1)
    filled = jnp.sum(jnp.where(place == spots, source - NP, 0.0), axis=0, keepdims=True)

    level = jnp.minimum(counts, LEVELS + 1.0)
    level = jnp.where(lax.broadcasted_iota(jnp.int32, (8, 256), 1) < NP, level, -1.0)
    across = jnp.broadcast_to(level[0:1], (256, 256))
    down = across.T
    ahead = (across > down) | ((across == down) & (col < row))
    spot = jnp.sum(jnp.where(ahead, 1.0, 0.0), axis=1, keepdims=True).astype(jnp.int32)
    order = jnp.sum(jnp.where(spot == col, row, 0).astype(f32), axis=0, keepdims=True)
    order = jnp.minimum(order, float(NP))
    tables[0:1, :] = (filled + NP).astype(jnp.int32)
    tables[1:2, 0:256] = start[0:1].astype(jnp.int32)
    tables[2:3, 0:256] = order.astype(jnp.int32)


def entries(quads, count):
    smem = pl.BlockSpec(memory_space=pltpu.SMEM)
    vmem = pl.BlockSpec(memory_space=pltpu.VMEM)
    return pl.pallas_call(
        entries_kernel,
        out_shape=[
            jax.ShapeDtypeStruct((8, CAPE + 128), jnp.int32),
            jax.ShapeDtypeStruct((NP, NP), jnp.float32),
        ],
        in_specs=[vmem, smem],
        out_specs=[vmem, vmem],
        cost_estimate=pl.CostEstimate(flops=10000, bytes_accessed=10000, transcendentals=0),
        name="sort_entries",
    )(quads, count)


def split(t):
    x = (t * 171) >> 11
    return x, t - x * T


def slot_of(direct, slots, t):
    if direct:
        return t
    x, y = split(t)
    z = (x * 11) >> 5
    return (x - 3 * z) * 64 + z * 16 + ((y * 11) >> 5) * 4 + slots[y]


def compute_kernel(direct, ids, slots, tables, core, coul, recv, factors, outbound,
                   dens, fac, fact, pw, ha, hb, corem, pot, cma, cmb, rha, rhb, in_sem, fac_sem, out_sem):
    for x in range(T):
        pltpu.make_async_copy(factors.at[ids[x]], fac.at[x], fac_sem).start()
    for x in range(T):
        def fetch(y, c, x=x):
            pltpu.make_async_copy(recv.at[slot_of(direct, slots, x * T + y)], dens.at[x * T + y], in_sem.at[x]).start()
            return c
        lax.fori_loop(0, T, fetch, 0)
    corem[...] = core[...] * -0.5
    pw[NP] = jnp.zeros((R, R), jnp.bfloat16)
    pltpu.make_async_copy(factors.at[pl.ds(0, T)], fac, fac_sem).wait()
    for x in range(T):
        fact[x] = fac[x].T

    eye = lax.broadcasted_iota(jnp.int32, (BS, BS), 0) == lax.broadcasted_iota(jnp.int32, (BS, BS), 1)

    def halves(x, hs):
        pltpu.make_async_copy(recv.at[pl.ds(0, T)], dens.at[pl.ds(0, T)], in_sem.at[x]).wait()
        fx = fac[x]
        for yp in range(T // 2):
            s = x * T + 2 * yp
            d2 = jnp.concatenate([dens[s], dens[s + 1]], axis=1)
            hs[yp] = jnp.dot(fx, d2, preferred_element_type=jnp.float32).astype(jnp.bfloat16)

    def pairs_of(x, hs):
        for y in range(T):
            s = x * T + y
            h = hs[y // 2, :, (y % 2) * BS:(y % 2 + 1) * BS]
            p = jnp.dot(h, fact[y], preferred_element_type=jnp.float32)
            pw[s] = p.astype(jnp.bfloat16)
            dia = [
                jnp.sum(jnp.where(eye, p[k * BS:(k + 1) * BS, k * BS:(k + 1) * BS], 0.0), axis=0, keepdims=True)
                for k in range(3)
            ]
            pot[s] = jnp.concatenate(dia, axis=1)

    halves(0, ha)

    def both(k, c):
        halves(2 * k + 1, hb)
        pairs_of(2 * k, ha)
        halves(2 * k + 2, ha)
        pairs_of(2 * k + 1, hb)
        return c

    lax.fori_loop(0, T // 2 - 1, both, 0)
    halves(T - 1, hb)
    pairs_of(T - 2, ha)
    pairs_of(T - 1, hb)
    pair_diag = pot[...].reshape(NP, R)
    total = jnp.dot(coul[...], pair_diag, precision=lax.Precision.HIGHEST, preferred_element_type=jnp.float32)
    pot[...] = jnp.dot(total, core[...], precision=lax.Precision.HIGHEST, preferred_element_type=jnp.float32).reshape(NP, 1, R)

    def source(lo, n, e):
        return jnp.where(e < n, tables[0, lo + e], NP)

    def entry(lo, n, e, rows):
        return pw[source(lo, n, e), rows].astype(jnp.float32)

    def entries_at(lo, n, e, many, rows):
        one = pw[source(lo, n, e), rows]
        if many == 2:
            one = one + pw[source(lo, n, e + 1), rows]
        return one.astype(jnp.float32)

    def put_core_matrices(ts, cms, count, extra, rows):
        r = rows.start
        block = r // BS
        at = r % BS
        weight = corem[rows]
        mask = eye[at:at + STRIP]
        for q, t in enumerate(ts):
            lo = tables[1, t]
            n = tables[1, t + 1] - lo
            dia = jnp.where(mask, pot[t, :, block * BS:(block + 1) * BS], 0.0)
            cols3 = [jnp.zeros((STRIP, BS), jnp.float32)] * 3
            if count:
                es = entries_at(lo, n, 0, min(2, count), rows)
                for k in range(2, count, 2):
                    es = es + entries_at(lo, n, k, min(2, count - k), rows)
                if extra:
                    es = lax.fori_loop(count, n, lambda k, v: v + entry(lo, n, k, rows), es)
                cm = weight * es
                cols3 = [cm[:, j * BS:(j + 1) * BS] for j in range(3)]
            cols3[block] = cols3[block] + dia
            cms[q, rows] = jnp.concatenate(cols3, axis=1).astype(jnp.bfloat16)

    def step(i, cm_now, cm_before, rh_now, rh_before):

        def ranked(j):
            return jnp.where(j >= 0, tables[2, jnp.maximum(j, 0)], NP)

        tg = [ranked(i * G + q) for q in range(G)]
        t1 = [ranked((i - 1) * G + q) for q in range(G)]
        t2 = [ranked((i - 2) * G + q) for q in range(G)]

        def late(q):
            x2, _ = split(jnp.minimum(t2[q], NP - 1))
            _, y1 = split(t1[q])
            dens[t2[q]] = jnp.dot(fact[x2], rh_before[q], preferred_element_type=jnp.float32).astype(jnp.bfloat16)
            rh_now[q] = jnp.dot(
                cm_before[q], fac[y1], preferred_element_type=jnp.float32
            ).astype(jnp.bfloat16)

        def branch(count, extra):
            def run():
                strips = R // STRIP
                for part in range(strips):
                    for q in range(part * G // strips, (part + 1) * G // strips):
                        late(q)
                    if count is not None:
                        put_core_matrices(tg, cm_now, count, extra, slice(part * STRIP, (part + 1) * STRIP))
            return run

        top = tables[1, tg[0] + 1] - tables[1, tg[0]]
        top = jnp.where(i < NP // G, top, -1)
        lax.switch(
            jnp.minimum(top, LEVELS + 1) + 1,
            [branch(None, False)] + [branch(k, False) for k in range(LEVELS + 1)] + [branch(LEVELS, True)],
        )
        @pl.when(i >= 2)
        def _():
            for q in range(G):
                pltpu.make_async_copy(dens.at[t2[q]], outbound.at[slot_of(direct, slots, t2[q])], out_sem).start()

    def steps(k, c):
        step(2 * k, cma, cmb, rha, rhb)
        step(2 * k + 1, cmb, cma, rhb, rha)
        return c

    lax.fori_loop(0, (NP // G + 2) // 2, steps, 0)
    pltpu.make_async_copy(dens.at[pl.ds(0, NP)], outbound.at[pl.ds(0, NP)], out_sem).wait()


def compute(ids, slots, tables, core, coul, recv, factors, nslots, direct=False):
    smem = pl.BlockSpec(memory_space=pltpu.SMEM)
    vmem = pl.BlockSpec(memory_space=pltpu.VMEM)
    hbm = pl.BlockSpec(memory_space=pl.ANY)
    return pl.pallas_call(
        functools.partial(compute_kernel, direct),
        out_shape=jax.ShapeDtypeStruct((nslots, BS, BS), jnp.bfloat16),
        in_specs=[smem] * 3 + [vmem] * 2 + [hbm] * 2,
        out_specs=hbm,
        scratch_shapes=[
            pltpu.VMEM((NP + 1, BS, BS), jnp.bfloat16),
            pltpu.VMEM((T, R, BS), jnp.bfloat16),
            pltpu.VMEM((T, BS, R), jnp.bfloat16),
            pltpu.VMEM((NP + 1, R, R), jnp.bfloat16),
            pltpu.VMEM((T // 2, R, 2 * BS), jnp.bfloat16),
            pltpu.VMEM((T // 2, R, 2 * BS), jnp.bfloat16),
            pltpu.VMEM((R, R), jnp.float32),
            pltpu.VMEM((NP, 1, R), jnp.float32),
            pltpu.VMEM((G, R, R), jnp.bfloat16),
            pltpu.VMEM((G, R, R), jnp.bfloat16),
            pltpu.VMEM((G, R, BS), jnp.bfloat16),
            pltpu.VMEM((G, R, BS), jnp.bfloat16),
            pltpu.SemaphoreType.DMA((T,)),
            pltpu.SemaphoreType.DMA,
            pltpu.SemaphoreType.DMA,
        ],
        compiler_params=pltpu.CompilerParams(vmem_limit_bytes=59 * 2**20),
        cost_estimate=pl.CostEstimate(flops=25 * 10**9, bytes_accessed=12 * 10**6, transcendentals=0),
        name="fock_pieces_direct" if direct else "fock_pieces",
    )(ids, slots, tables, core, coul, recv, factors)


CAP = 9
RELAY = 144
MESH = pl.DeviceIdType.MESH
ORDERS = ((2, 1, 0), (1, 0, 2), (0, 2, 1))


def line_of(u):
    chip = [(v * 43) >> 8 for v in u]
    col = [v - 6 * q for v, q in zip(u, chip)]
    e01 = chip[0] == chip[1]
    e02 = chip[0] == chip[2]
    e12 = chip[1] == chip[2]
    twice = e01 | e02 | e12
    over1 = e01
    over2 = e02 | e12
    where2 = jnp.where(e12, chip[1], chip[0])
    over_col = jnp.where(e01, col[1], col[2])
    third = jnp.where(e01, chip[2], jnp.where(e02, chip[1], chip[0]))
    rel = (third - where2) & 3
    return chip, col, twice, over1, over2, where2, over_col, rel


def route_kernel(place, ids, tab, lists, idt, plus_s, minus_s, rankp_s, rankm_s):
    z, y, x, c = place[0], place[1], place[2], place[3]
    idt[...] = ids[...].astype(jnp.float32).T.astype(jnp.int32)
    lane = lax.broadcasted_iota(jnp.int32, (1, 128), 1)
    rows8 = lax.broadcasted_iota(jnp.int32, (8, 128), 0)
    lanes8 = lax.broadcasted_iota(jnp.int32, (8, 128), 1)
    f32 = jnp.float32
    below = (
        lax.broadcasted_iota(jnp.int32, (128, 128), 0) < lax.broadcasted_iota(jnp.int32, (128, 128), 1)
    ).astype(f32).astype(jnp.bfloat16)

    def prefix(m):
        return jnp.dot(m.astype(jnp.bfloat16), below, preferred_element_type=f32)

    lines = []
    fp, fm, fl = [], [], []
    for g in range(4):
        u = [idt[3 * g + j:3 * g + j + 1, :] - 24 * g for j in range(3)]
        ln = line_of(u)
        lines.append(ln)
        chip, col, twice, over1, over2, where2, over_col, rel = ln
        kind = jnp.where(twice, rel, 0)
        at = jnp.broadcast_to(where2, (8, 128)) == rows8 // 2
        here = at & ((lanes8 & 1) == (rows8 & 1))
        kind8 = jnp.broadcast_to(kind, (8, 128))
        fp.append(jnp.where(here & (kind8 == 3), 1.0, 0.0))
        fm.append(jnp.where(here & (kind8 == 1), 1.0, 0.0))
        fl.append(jnp.where(here & (kind8 == 2), 1.0, 0.0))
    fp = jnp.concatenate(fp, axis=0)
    fm = jnp.concatenate(fm, axis=0)
    fl = jnp.concatenate(fl, axis=0)
    np_ = jnp.sum(fp, axis=1, keepdims=True)
    nm_ = jnp.sum(fm, axis=1, keepdims=True)
    nl_ = jnp.sum(fl, axis=1, keepdims=True)
    give = jnp.clip(jnp.floor((nl_ + nm_ - np_ + 1.0) * 0.5), 0.0, nl_)
    first = fl * jnp.where(prefix(fl) < give, 1.0, 0.0)
    plus = fp + first
    minus = fm + fl - first
    plus_s[...] = plus
    minus_s[...] = minus
    rankp_s[...] = prefix(plus)
    rankm_s[...] = prefix(minus)
    most = jnp.max(jnp.maximum(jnp.sum(plus, axis=1, keepdims=True), jnp.sum(minus, axis=1, keepdims=True)), axis=0, keepdims=True)

    me = ((z * 4 + y) * 4 + x) * 2 + c
    own = jnp.zeros((1, 128), jnp.int32)
    for g in range(4):
        chip, col, twice, over1, over2, where2, over_col, rel = lines[g]
        goes = jnp.sum(plus[8 * g:8 * g + 8], axis=0, keepdims=True) > 0.5
        to = (where2 + jnp.where(goes, 1, 3)) & 3
        slots = [chip[0], jnp.where(over1, to, chip[1]), jnp.where(over2, to, chip[2])]
        for j in range(3):
            mine = jnp.sum(jnp.where(lane == me, slots[j], 0).astype(f32), axis=1, keepdims=True)
            own = own + jnp.where(lane == 3 * g + j, mine.astype(jnp.int32), 0)
    own = own + jnp.where(lane == 127, (most > CAP + 0.5).astype(jnp.int32), 0)

    u = [idt[pl.ds(3 * y + j, 1), :] - 24 * y for j in range(3)]
    chip, col, twice, over1, over2, where2, over_col, rel = line_of(u)
    rk = [idt[pl.ds(3 * z + k, 1), :] - 24 * z for k in range(3)]
    line_row = y * 8 + x * 2 + c
    left_row = y * 8 + ((x + 3) & 3) * 2 + c
    right_row = y * 8 + ((x + 1) & 3) * 2 + c

    def pool_col(v):
        core = jnp.where(v >= 3, 1, 0)
        return jnp.where(core == c, 0, 72) + v - 3 * core

    main = jnp.full((1, 128), -1, jnp.int32)
    for j, over in enumerate((chip[0] < 0, over1, over2)):
        main = jnp.where((chip[j] == x) & jnp.logical_not(over), pool_col(col[j]), main)
    from_left = plus_s[pl.ds(left_row, 1), :] > 0.5
    rank_left = rankp_s[pl.ds(left_row, 1), :].astype(jnp.int32)
    from_right = minus_s[pl.ds(right_row, 1), :] > 0.5
    rank_right = rankm_s[pl.ds(right_row, 1), :].astype(jnp.int32)
    for k in range(3):
        idx = jnp.where(main >= 0, main + rk[k] * 3, -1)
        idx = jnp.where(from_left, RELAY + rank_left, idx)
        idx = jnp.where(from_right, RELAY + CAP + rank_right, idx)
        tab[k:k + 1, :] = idx
    tab[3:7, :] = jnp.zeros((4, 128), jnp.int32)
    tab[7:8, :] = own

    j16 = lax.broadcasted_iota(jnp.int32, (16, 128), 0)
    l16 = lax.broadcasted_iota(jnp.int32, (16, 128), 1)
    out = jnp.zeros((16, 128), jnp.int32)

    def listed(flag, rank, value):
        sel = jnp.broadcast_to(flag, (16, 128)) & (jnp.broadcast_to(rank, (16, 128)) == j16)
        got = jnp.sum(jnp.where(sel, jnp.broadcast_to(value, (16, 128)) + 1, 0).astype(f32), axis=1, keepdims=True)
        return got.astype(jnp.int32) - 1

    my_plus = plus_s[pl.ds(line_row, 1), :] > 0.5
    my_rankp = rankp_s[pl.ds(line_row, 1), :].astype(jnp.int32)
    my_minus = minus_s[pl.ds(line_row, 1), :] > 0.5
    my_rankm = rankm_s[pl.ds(line_row, 1), :].astype(jnp.int32)
    for k in range(3):
        value = pool_col(over_col) + rk[k] * 3
        out = jnp.where(l16 == k, listed(my_plus, my_rankp, value), out)
        out = jnp.where(l16 == 3 + k, listed(my_minus, my_rankm, value), out)
    out = jnp.where(l16 == 6, listed(from_left, rank_left, lane), out)
    out = jnp.where(l16 == 7, listed(from_right, rank_right, lane), out)
    lists[...] = out


def route(place, ids):
    smem = pl.BlockSpec(memory_space=pltpu.SMEM)
    vmem = pl.BlockSpec(memory_space=pltpu.VMEM)
    return pl.pallas_call(
        route_kernel,
        out_shape=[jax.ShapeDtypeStruct((8, 128), jnp.int32), jax.ShapeDtypeStruct((16, 128), jnp.int32)],
        in_specs=[smem, vmem],
        out_specs=[vmem, vmem],
        scratch_shapes=[pltpu.VMEM((128, 128), jnp.int32)] + [pltpu.VMEM((32, 128), jnp.float32)] * 4,
        name="route_tasks",
    )(place, ids)


def here():
    z = lax.axis_index("row")
    b = lax.axis_index("bulk")
    return b // 2 % 4, b // 8, z, b % 2


def device(x, y, z, c):
    return (z, y * 8 + x * 2 + c)


def moved(at, axis, by):
    pos = list(at[:3])
    pos[axis] = lax.rem(pos[axis] + by, 4)
    return device(*pos, at[3])


def greet(at):
    barrier = pltpu.get_barrier_semaphore()
    for axis in range(3):
        for by in (1, 2, 3):
            pl.semaphore_signal(barrier, inc=1, device_id=moved(at, axis, by), device_id_type=MESH)
    pl.semaphore_wait(barrier, 9)


def part(ref, axis, index):
    if axis == 2:
        return ref.at[index]
    if axis == 1:
        return ref.at[:, index]
    return ref.at[:, :, index]


def phase_copies(at, k, step, src, dst, send, recv, local):
    axis = ORDERS[k][step]
    own = at[axis]
    copies = [pltpu.make_async_copy(part(src, axis, own), part(dst, axis, own), local.at[k, step])]
    for by in (1, 2, 3):
        to = lax.rem(own + by, 4)
        copies.append(
            pltpu.make_async_remote_copy(
                part(src, axis, to), part(dst, axis, own),
                send.at[k, step, by - 1], recv.at[k, step, by - 1],
                device_id=moved(at, axis, by), device_id_type=MESH,
            )
        )
    return copies


def start_all(copies):
    for copy in copies:
        copy.start()


def wait_all(copies):
    for copy in copies:
        copy.wait()


def share_kernel(mine, density, ids, sibling, buf, line, send, recv, swap_send, swap_recv):
    at = here()
    x, y, z, c = at
    barrier = pltpu.get_barrier_semaphore()
    for axis in range(3):
        for by in (1, 2, 3):
            pl.semaphore_signal(barrier, inc=1, device_id=moved(at, axis, by), device_id_type=MESH)
    pl.semaphore_signal(barrier, inc=1, device_id=device(x, y, z, 1 - c), device_id_type=MESH)
    line[...] = jnp.zeros_like(line)
    line[:, :T] = mine[...]
    buf[z, y, x, c] = line[...]
    pl.semaphore_wait(barrier, 10)
    swap = pltpu.make_async_remote_copy(
        density, sibling, swap_send, swap_recv, device_id=device(x, y, z, 1 - c), device_id_type=MESH
    )
    pair = pltpu.make_async_remote_copy(
        buf.at[z, y, x, c], buf.at[z, y, x, c], send.at[9], recv.at[9],
        device_id=device(x, y, z, 1 - c), device_id_type=MESH,
    )
    pair.start()
    pair.wait()
    swap.start()
    for axis, held in ((0, buf.at[z, y, x]), (1, buf.at[z, y]), (2, buf.at[z])):
        copies = [
            pltpu.make_async_remote_copy(
                held, held, send.at[3 * axis + by - 1], recv.at[3 * axis + by - 1],
                device_id=moved(at, axis, by), device_id_type=MESH,
            )
            for by in (1, 2, 3)
        ]
        start_all(copies)
        wait_all(copies)
    for d in range(128):
        ids[d:d + 1, :] = buf[d // 32, d // 8 % 4, d // 2 % 4, d % 2]
    swap.wait()


def share_tasks(mine, density):
    vmem = pl.BlockSpec(memory_space=pltpu.VMEM)
    hbm = pl.BlockSpec(memory_space=pl.ANY)
    dma = pltpu.SemaphoreType.DMA
    return pl.pallas_call(
        share_kernel,
        out_shape=[jax.ShapeDtypeStruct((128, 128), jnp.int32), jax.ShapeDtypeStruct((72, BS, BS), jnp.bfloat16)],
        in_specs=[vmem, hbm],
        out_specs=[vmem, hbm],
        scratch_shapes=[pltpu.VMEM((4, 4, 4, 2, 1, 128), jnp.int32), pltpu.VMEM((1, 128), jnp.int32)]
        + [dma((10,)), dma((10,)), dma, dma],
        compiler_params=pltpu.CompilerParams(collective_id=3, has_side_effects=True),
        name="share_tasks",
    )(mine, density.reshape(72, BS, BS))


def fetch_kernel(tab, lists, density, sibling, out, pool, r0, r1, r2, rs, a, b, d,
                 load, relay_send, relay_recv, send, recv, local):
    at = here()
    c = at[3]
    mine = pltpu.make_async_copy(density, pool.at[pl.ds(0, 72)], load.at[0])
    other = pltpu.make_async_copy(sibling, pool.at[pl.ds(72, 72)], load.at[1])
    mine.start()
    other.start()
    greet(at)
    mine.wait()
    other.wait()
    relayed = (r0, r1, r2)
    relays = []
    for k in range(3):
        def fill(j, cc, k=k):
            rs[k, j] = pool[jnp.maximum(lists[j, k], 0)]
            rs[k, CAP + j] = pool[jnp.maximum(lists[j, 3 + k], 0)]
            return cc
        lax.fori_loop(0, CAP, fill, 0)
        pair = [
            pltpu.make_async_remote_copy(
                rs.at[k, pl.ds(CAP * side, CAP)], relayed[k].at[pl.ds(CAP * side, CAP)],
                relay_send.at[k, side], relay_recv.at[k, side],
                device_id=moved(at, 0, 1 if side == 0 else 3), device_id_type=MESH,
            )
            for side in range(2)
        ]
        start_all(pair)
        relays.append(pair)
    steps = []
    for k in range(3):
        wait_all(relays[k])

        def fill(i, cc, k=k):
            index = tab[k, 2 * i + c]
            plain = pool[jnp.clip(index, 0, 143)]
            passed = relayed[k][jnp.clip(index - RELAY, 0, 2 * CAP - 1)]
            a[k, i // 16, i // 4 % 4, i % 4] = jnp.where(index >= RELAY, passed, plain)
            return cc

        lax.fori_loop(0, 64, fill, 0)
        copies = phase_copies(at, k, 0, a.at[k], b.at[k], send, recv, local)
        start_all(copies)
        steps.append(copies)
    for step, src, dst in ((1, b, d), (2, d, out)):
        for k in range(3):
            wait_all(steps[k])
            copies = phase_copies(at, k, step, src.at[k], dst.at[k], send, recv, local)
            start_all(copies)
            steps[k] = copies
    for k in range(3):
        wait_all(steps[k])


def fetch_blocks(tab, lists, density, sibling):
    smem = pl.BlockSpec(memory_space=pltpu.SMEM)
    hbm = pl.BlockSpec(memory_space=pl.ANY)
    cube = pltpu.VMEM((3, 4, 4, 4, BS, BS), jnp.bfloat16)
    dma = pltpu.SemaphoreType.DMA
    return pl.pallas_call(
        fetch_kernel,
        out_shape=jax.ShapeDtypeStruct((3, 4, 4, 4, BS, BS), jnp.bfloat16),
        in_specs=[smem, smem, hbm, hbm],
        out_specs=hbm,
        scratch_shapes=[pltpu.VMEM((144, BS, BS), jnp.bfloat16)]
        + [pltpu.VMEM((2 * CAP, BS, BS), jnp.bfloat16)] * 3
        + [pltpu.VMEM((3, 2 * CAP, BS, BS), jnp.bfloat16), cube, cube, cube]
        + [dma((2,)), dma((3, 2)), dma((3, 2)), dma((3, 3, 3)), dma((3, 3, 3)), dma((3, 3))],
        compiler_params=pltpu.CompilerParams(
            collective_id=1, has_side_effects=True, vmem_limit_bytes=50 * 2**20
        ),
        name="fetch_blocks",
    )(tab, lists, density.reshape(72, BS, BS), sibling.reshape(72, BS, BS))


def return_kernel(lists, pieces, out, back, b, d, e0, e1, e2, rs,
                  relay_send, relay_recv, send, recv, local, store):
    at = here()
    greet(at)
    ends = (e0, e1, e2)
    steps = []
    for k in range(3):
        copies = phase_copies(at, k, 0, pieces.at[k], b.at[k], send, recv, local)
        start_all(copies)
        steps.append(copies)
    for k in range(3):
        wait_all(steps[k])
        steps[k] = phase_copies(at, k, 1, b.at[k], d.at[k], send, recv, local)
        start_all(steps[k])
    for k in range(3):
        wait_all(steps[k])
        steps[k] = phase_copies(at, k, 2, d.at[k], ends[k], send, recv, local)
        start_all(steps[k])
    for k in range(3):
        wait_all(steps[k])
        kept = pltpu.make_async_copy(ends[k], out.at[k], store.at[k])
        kept.start()

        def fill(j, cc, k=k):
            for side in range(2):
                t = jnp.maximum(lists[j, 6 + side], 0) // 2
                rs[k, side * CAP + j] = ends[k][t // 16, t // 4 % 4, t % 4]
            return cc

        lax.fori_loop(0, CAP, fill, 0)
        pair = [
            pltpu.make_async_remote_copy(
                rs.at[k, pl.ds(CAP * side, CAP)], back.at[k, pl.ds(CAP * side, CAP)],
                relay_send.at[k, side], relay_recv.at[k, side],
                device_id=moved(at, 0, 3 if side == 0 else 1), device_id_type=MESH,
            )
            for side in range(2)
        ]
        start_all(pair)
        steps[k] = pair + [kept]
    for k in range(3):
        wait_all(steps[k])


def return_pieces(lists, pieces):
    smem = pl.BlockSpec(memory_space=pltpu.SMEM)
    hbm = pl.BlockSpec(memory_space=pl.ANY)
    cube = pltpu.VMEM((3, 4, 4, 4, BS, BS), jnp.bfloat16)
    dma = pltpu.SemaphoreType.DMA
    return pl.pallas_call(
        return_kernel,
        out_shape=[
            jax.ShapeDtypeStruct((3, 4, 4, 4, BS, BS), jnp.bfloat16),
            jax.ShapeDtypeStruct((3, 2 * CAP, BS, BS), jnp.bfloat16),
        ],
        in_specs=[smem, hbm],
        out_specs=[hbm, hbm],
        scratch_shapes=[cube, cube]
        + [pltpu.VMEM((4, 4, 4, BS, BS), jnp.bfloat16)] * 3
        + [pltpu.VMEM((3, 2 * CAP, BS, BS), jnp.bfloat16)]
        + [dma((3, 2)), dma((3, 2)), dma((3, 3, 3)), dma((3, 3, 3)), dma((3, 3)), dma((3,))],
        compiler_params=pltpu.CompilerParams(
            collective_id=2, has_side_effects=True, vmem_limit_bytes=50 * 2**20
        ),
        name="return_pieces",
    )(lists, pieces)


def collect_kernel(place, tab, lists, got, back, own, other, acc):
    c = place[3]
    acc[...] = jnp.zeros_like(acc)
    own[...] = jnp.zeros_like(own)

    def put(index, block):
        @pl.when((index >= 0) & (index < 72))
        def _():
            own[jnp.clip(index, 0, 71)] += block().astype(jnp.float32)

        @pl.when((index >= 72) & (index < 144))
        def _():
            acc[jnp.clip(index - 72, 0, 71)] += block().astype(jnp.float32)

    def add(i, cc):
        for k in range(3):
            put(tab[k, 2 * i + c], lambda: got[k, i])
        return cc

    lax.fori_loop(0, 64, add, 0)

    def add_back(j, cc):
        for k in range(3):
            for side in range(2):
                put(lists[j, 3 * side + k], lambda: back[k, side * CAP + j])
        return cc

    lax.fori_loop(0, CAP, add_back, 0)
    other[...] = acc[...].astype(jnp.bfloat16)


def collect(place, tab, lists, got, back):
    smem = pl.BlockSpec(memory_space=pltpu.SMEM)
    vmem = pl.BlockSpec(memory_space=pltpu.VMEM)
    return pl.pallas_call(
        collect_kernel,
        out_shape=[
            jax.ShapeDtypeStruct((72, BS, BS), jnp.float32),
            jax.ShapeDtypeStruct((72, BS, BS), jnp.bfloat16),
        ],
        in_specs=[smem, smem, smem, vmem, vmem],
        out_specs=[vmem, vmem],
        scratch_shapes=[pltpu.VMEM((72, BS, BS), jnp.float32)],
        compiler_params=pltpu.CompilerParams(vmem_limit_bytes=50 * 2**20),
        name="collect_pieces",
    )(place, tab, lists, got.reshape(3, 64, BS, BS), back)


def swap_cores(value):
    return lax.ppermute(value, "bulk", [(i, i ^ 1) for i in range(32)])


def fast_path(density, factors, core, mine, sibling, tables, place, tab, lists, coul):
    recv = fetch_blocks(tab, lists, density, sibling).reshape(192, BS, BS)
    pieces = compute(mine, tab[7], tables, core, coul, recv, factors, 192)
    got, back = return_pieces(lists, pieces.reshape(3, 4, 4, 4, BS, BS))
    own, other = collect(place, tab, lists, got, back)
    return (own + swap_cores(other).astype(jnp.float32)).reshape(24, 3, BS, BS)


def column_of(ids, d, bulk):
    group = bulk // 8
    local = jnp.int32(-1)
    for j in range(3):
        block = ids[d * T + group * 3 + j]
        local = jnp.where(block // 3 == bulk, block % 3, local)
    return local


def pack_kernel(place, ids, density, out, sem):
    row = place[0]
    bulk = place[1]

    def copy(d, j, col):
        r = ids[d * T + row * 3 + j] - row * 24
        return pltpu.make_async_copy(density.at[r, col], out.at[d * 3 + j], sem)

    def send(d, n):
        col = column_of(ids, d, bulk)

        @pl.when(col >= 0)
        def _():
            for j in range(3):
                copy(d, j, col).start()

        return n + (col >= 0).astype(jnp.int32)

    n = lax.fori_loop(0, 128, send, 0)

    def drain(i, c):
        pltpu.make_async_copy(out.at[pl.ds(0, 3)], out.at[pl.ds(0, 3)], sem).wait()
        return c

    lax.fori_loop(0, n, drain, 0)


def pack(place, ids, density):
    smem = pl.BlockSpec(memory_space=pltpu.SMEM)
    hbm = pl.BlockSpec(memory_space=pl.ANY)
    return pl.pallas_call(
        pack_kernel,
        out_shape=jax.ShapeDtypeStruct((384, BS, BS), jnp.bfloat16),
        in_specs=[smem, smem, hbm],
        out_specs=hbm,
        scratch_shapes=[pltpu.SemaphoreType.DMA],
        name="pack_density",
    )(place, ids, density)


def gather_kernel(place, ids, inbound, fock, buf, sems):
    row = place[0]
    bulk = place[1]

    def fetch(d, c):
        @pl.when(column_of(ids, d, bulk) >= 0)
        def _():
            pltpu.make_async_copy(inbound.at[pl.ds(d * 3, 3)], buf.at[pl.ds(d * 3, 3)], sems.at[d]).start()

        return c

    lax.fori_loop(0, 128, fetch, 0)
    fock[...] = jnp.zeros_like(fock)

    def add(d, c):
        col = column_of(ids, d, bulk)

        @pl.when(col >= 0)
        def _():
            pltpu.make_async_copy(inbound.at[pl.ds(d * 3, 3)], buf.at[pl.ds(d * 3, 3)], sems.at[d]).wait()
            for j in range(3):
                r = ids[d * T + row * 3 + j] - row * 24
                fock[r, col] += buf[d * 3 + j].astype(jnp.float32)

        return c

    lax.fori_loop(0, 128, add, 0)


def gather(place, ids, inbound):
    smem = pl.BlockSpec(memory_space=pltpu.SMEM)
    vmem = pl.BlockSpec(memory_space=pltpu.VMEM)
    hbm = pl.BlockSpec(memory_space=pl.ANY)
    return pl.pallas_call(
        gather_kernel,
        out_shape=jax.ShapeDtypeStruct((24, 3, BS, BS), jnp.float32),
        in_specs=[smem, smem, hbm],
        out_specs=vmem,
        scratch_shapes=[pltpu.VMEM((384, BS, BS), jnp.bfloat16), pltpu.SemaphoreType.DMA((128,))],
        compiler_params=pltpu.CompilerParams(vmem_limit_bytes=40 * 2**20),
        name="add_pieces",
    )(place, ids, inbound)


def slow_path(density, factors, core, mine, tables, place, ids, coul):
    axes = ("row", "bulk")
    where = jnp.stack([place[0], place[1] * 8 + place[2] * 2 + place[3]])
    ids = ids[:, :T].reshape(-1)
    sent = pack(where, ids, density)
    recv = lax.all_to_all(sent, axes, split_axis=0, concat_axis=0, tiled=True)
    owner = mine[:, None] // 24 * 32 + mine[None, :] // 3
    slot = (owner * 3 + (jnp.arange(T) % 3)[:, None]).reshape(-1)
    pieces = compute(mine, mine, tables, core, coul, recv[slot], factors, NP, direct=True)
    outbound = jnp.zeros((384, BS, BS), jnp.bfloat16).at[slot].set(pieces)
    inbound = lax.all_to_all(outbound, axes, split_axis=0, concat_axis=0, tiled=True)
    return gather(where, ids, inbound)


def shards(density, factors, core, task_blocks, quartets, quartet_count):
    mine = task_blocks[0]
    bulk = lax.axis_index("bulk")
    place = jnp.stack([lax.axis_index("row"), bulk // 8, bulk // 2 % 4, bulk % 2]).astype(jnp.int32)
    ids, sibling = share_tasks(task_blocks, density)
    tables, coul = entries(quartets, quartet_count)
    tab, lists = route(place, ids)
    fock = fast_path(density, factors, core, mine, sibling, tables, place, tab, lists, coul)

    def again(state):
        return state[0]

    def padded(state):
        return jnp.array(False), slow_path(density, factors, core, mine, tables, place, ids, coul)

    return lax.while_loop(again, padded, (tab[7, 127] > 0, fock))[1]


def solution(mesh):
    return jax.shard_map(
        shards,
        mesh=mesh,
        in_specs=(
            P("row", "bulk", None, None),
            P(),
            P(),
            P(("row", "bulk"), None),
            P(("row", "bulk"), None),
            P(("row", "bulk")),
        ),
        out_specs=P("row", "bulk", None, None),
        check_vma=False,
    )
```

```python
import functools

import jax
import jax.numpy as jnp
from jax import lax
from jax.experimental import pallas as pl
from jax.experimental.pallas import tpu as pltpu
from jax.sharding import PartitionSpec as P

T = 12
NP = 144
R = 384
BS = 128
CAPE = 512
G = 4
LEVELS = 7
STRIP = 64


def entries_kernel(quads, count, tables, coul):
    f32 = jnp.float32
    live = lax.broadcasted_iota(jnp.int32, (128, 1), 0) < count[0]
    q = jnp.concatenate([quads[...], jnp.zeros((4, 128), jnp.int32)], axis=0).astype(f32).T.astype(jnp.int32)
    a, b, c, e = (q[:, n:n + 1] for n in range(4))
    lanes = lax.broadcasted_iota(jnp.int32, (128, 256), 1)

    def hot(t):
        return jnp.where((t == lanes) & live, 1.0, 0.0)

    def product(u, v):
        return jnp.dot(u.T.astype(jnp.bfloat16), v.astype(jnp.bfloat16), preferred_element_type=f32)

    bra = hot(a * T + b)
    ket = hot(c * T + e)
    table = 2.0 * (product(bra, ket) + product(ket, bra))
    coul[...] = table[:NP, :NP]

    targets = [a * T + c, a * T + e, b * T + c, b * T + e]
    sources = [b * T + e, b * T + c, a * T + e, a * T + c]
    member = jnp.concatenate([hot(t) for t in targets], axis=0)
    source = jnp.concatenate(sources, axis=0).astype(f32)
    older = lax.broadcasted_iota(jnp.int32, (CAPE, CAPE), 0) > lax.broadcasted_iota(jnp.int32, (CAPE, CAPE), 1)
    rank = jnp.dot(
        jnp.where(older, 1.0, 0.0).astype(jnp.bfloat16), member.astype(jnp.bfloat16), preferred_element_type=f32
    )
    counts = jnp.broadcast_to(jnp.sum(member, axis=0, keepdims=True), (8, 256))
    row = lax.broadcasted_iota(jnp.int32, (256, 256), 0)
    col = lax.broadcasted_iota(jnp.int32, (256, 256), 1)
    start = jnp.dot(
        counts, jnp.where(row < col, 1.0, 0.0), precision=lax.Precision.HIGHEST, preferred_element_type=f32
    )
    used = jnp.sum(member, axis=1, keepdims=True) > 0.5
    place = jnp.sum(member * (rank + start[0:1]), axis=1, keepdims=True)
    place = jnp.where(used, place, -1.0).astype(jnp.int32)
    spots = lax.broadcasted_iota(jnp.int32, (CAPE, CAPE + 128), 1)
    filled = jnp.sum(jnp.where(place == spots, source - NP, 0.0), axis=0, keepdims=True)

    level = jnp.minimum(counts, LEVELS + 1.0)
    level = jnp.where(lax.broadcasted_iota(jnp.int32, (8, 256), 1) < NP, level, -1.0)
    across = jnp.broadcast_to(level[0:1], (256, 256))
    down = across.T
    ahead = (across > down) | ((across == down) & (col < row))
    spot = jnp.sum(jnp.where(ahead, 1.0, 0.0), axis=1, keepdims=True).astype(jnp.int32)
    order = jnp.sum(jnp.where(spot == col, row, 0).astype(f32), axis=0, keepdims=True)
    order = jnp.minimum(order, float(NP))
    tables[0:1, :] = (filled + NP).astype(jnp.int32)
    tables[1:2, 0:256] = start[0:1].astype(jnp.int32)
    tables[2:3, 0:256] = order.astype(jnp.int32)


def entries(quads, count):
    smem = pl.BlockSpec(memory_space=pltpu.SMEM)
    vmem = pl.BlockSpec(memory_space=pltpu.VMEM)
    return pl.pallas_call(
        entries_kernel,
        out_shape=[
            jax.ShapeDtypeStruct((8, CAPE + 128), jnp.int32),
            jax.ShapeDtypeStruct((NP, NP), jnp.float32),
        ],
        in_specs=[vmem, smem],
        out_specs=[vmem, vmem],
        cost_estimate=pl.CostEstimate(flops=10000, bytes_accessed=10000, transcendentals=0),
        name="sort_entries",
    )(quads.T, count)


def split(t):
    x = (t * 171) >> 11
    return x, t - x * T


def slot_of(direct, slots, t):
    if direct:
        return t
    x, y = split(t)
    z = (x * 11) >> 5
    return (x - 3 * z) * 64 + z * 16 + ((y * 11) >> 5) * 4 + slots[7, y]


def compute_kernel(direct, ids, slots, tables, core, coul, recv, factors, outbound,
                   dens, fac, fact, pw, ha, hb, corem, pot, cma, cmb, rha, rhb, in_sem, fac_sem, out_sem):
    for x in range(T):
        pltpu.make_async_copy(factors.at[ids[x]], fac.at[x], fac_sem).start()
    for x in range(T):
        def fetch(y, c, x=x):
            pltpu.make_async_copy(recv.at[slot_of(direct, slots, x * T + y)], dens.at[x * T + y], in_sem.at[x]).start()
            return c
        lax.fori_loop(0, T, fetch, 0)
    corem[...] = core[...] * -0.5
    pw[NP] = jnp.zeros((R, R), jnp.bfloat16)
    pltpu.make_async_copy(factors.at[pl.ds(0, T)], fac, fac_sem).wait()
    for x in range(T):
        fact[x] = fac[x].T

    eye = lax.broadcasted_iota(jnp.int32, (BS, BS), 0) == lax.broadcasted_iota(jnp.int32, (BS, BS), 1)

    def halves(x, hs):
        pltpu.make_async_copy(recv.at[pl.ds(0, T)], dens.at[pl.ds(0, T)], in_sem.at[x]).wait()
        fx = fac[x]
        for yp in range(T // 2):
            s = x * T + 2 * yp
            d2 = jnp.concatenate([dens[s], dens[s + 1]], axis=1)
            hs[yp] = jnp.dot(fx, d2, preferred_element_type=jnp.float32).astype(jnp.bfloat16)

    def pairs_of(x, hs):
        for y in range(T):
            s = x * T + y
            h = hs[y // 2, :, (y % 2) * BS:(y % 2 + 1) * BS]
            p = jnp.dot(h, fact[y], preferred_element_type=jnp.float32)
            pw[s] = p.astype(jnp.bfloat16)
            dia = [
                jnp.sum(jnp.where(eye, p[k * BS:(k + 1) * BS, k * BS:(k + 1) * BS], 0.0), axis=0, keepdims=True)
                for k in range(3)
            ]
            pot[s] = jnp.concatenate(dia, axis=1)

    halves(0, ha)

    def both(k, c):
        halves(2 * k + 1, hb)
        pairs_of(2 * k, ha)
        halves(2 * k + 2, ha)
        pairs_of(2 * k + 1, hb)
        return c

    lax.fori_loop(0, T // 2 - 1, both, 0)
    halves(T - 1, hb)
    pairs_of(T - 2, ha)
    pairs_of(T - 1, hb)
    pair_diag = pot[...].reshape(NP, R)
    total = jnp.dot(coul[...], pair_diag, precision=lax.Precision.HIGHEST, preferred_element_type=jnp.float32)
    pot[...] = jnp.dot(total, core[...], precision=lax.Precision.HIGHEST, preferred_element_type=jnp.float32).reshape(NP, 1, R)

    def source(lo, n, e):
        return jnp.where(e < n, tables[0, lo + e], NP)

    def entry(lo, n, e, rows):
        return pw[source(lo, n, e), rows].astype(jnp.float32)

    def entries_at(lo, n, e, many, rows):
        one = pw[source(lo, n, e), rows]
        if many == 2:
            one = one + pw[source(lo, n, e + 1), rows]
        return one.astype(jnp.float32)

    def put_core_matrices(ts, cms, count, extra, rows):
        r = rows.start
        block = r // BS
        at = r % BS
        weight = corem[rows]
        mask = eye[at:at + STRIP]
        for q, t in enumerate(ts):
            lo = tables[1, t]
            n = tables[1, t + 1] - lo
            dia = jnp.where(mask, pot[t, :, block * BS:(block + 1) * BS], 0.0)
            cols3 = [jnp.zeros((STRIP, BS), jnp.float32)] * 3
            if count:
                es = entries_at(lo, n, 0, min(2, count), rows)
                for k in range(2, count, 2):
                    es = es + entries_at(lo, n, k, min(2, count - k), rows)
                if extra:
                    es = lax.fori_loop(count, n, lambda k, v: v + entry(lo, n, k, rows), es)
                cm = weight * es
                cols3 = [cm[:, j * BS:(j + 1) * BS] for j in range(3)]
            cols3[block] = cols3[block] + dia
            cms[q, rows] = jnp.concatenate(cols3, axis=1).astype(jnp.bfloat16)

    def step(i, cm_now, cm_before, rh_now, rh_before):

        def ranked(j):
            return jnp.where(j >= 0, tables[2, jnp.maximum(j, 0)], NP)

        tg = [ranked(i * G + q) for q in range(G)]
        t1 = [ranked((i - 1) * G + q) for q in range(G)]
        t2 = [ranked((i - 2) * G + q) for q in range(G)]

        def late(q):
            x2, _ = split(jnp.minimum(t2[q], NP - 1))
            _, y1 = split(t1[q])
            dens[t2[q]] = jnp.dot(fact[x2], rh_before[q], preferred_element_type=jnp.float32).astype(jnp.bfloat16)
            rh_now[q] = jnp.dot(
                cm_before[q], fac[y1], preferred_element_type=jnp.float32
            ).astype(jnp.bfloat16)

        def branch(count, extra):
            def run():
                strips = R // STRIP
                for part in range(strips):
                    for q in range(part * G // strips, (part + 1) * G // strips):
                        late(q)
                    if count is not None:
                        put_core_matrices(tg, cm_now, count, extra, slice(part * STRIP, (part + 1) * STRIP))
            return run

        top = tables[1, tg[0] + 1] - tables[1, tg[0]]
        top = jnp.where(i < NP // G, top, -1)
        lax.switch(
            jnp.minimum(top, LEVELS + 1) + 1,
            [branch(None, False)] + [branch(k, False) for k in range(LEVELS + 1)] + [branch(LEVELS, True)],
        )
        @pl.when(i >= 2)
        def _():
            for q in range(G):
                pltpu.make_async_copy(dens.at[t2[q]], outbound.at[slot_of(direct, slots, t2[q])], out_sem).start()

    def steps(k, c):
        step(2 * k, cma, cmb, rha, rhb)
        step(2 * k + 1, cmb, cma, rhb, rha)
        return c

    lax.fori_loop(0, (NP // G + 2) // 2, steps, 0)
    pltpu.make_async_copy(dens.at[pl.ds(0, NP)], outbound.at[pl.ds(0, NP)], out_sem).wait()


def compute(ids, slots, tables, core, coul, recv, factors, nslots, direct=False):
    smem = pl.BlockSpec(memory_space=pltpu.SMEM)
    vmem = pl.BlockSpec(memory_space=pltpu.VMEM)
    hbm = pl.BlockSpec(memory_space=pl.ANY)
    return pl.pallas_call(
        functools.partial(compute_kernel, direct),
        out_shape=jax.ShapeDtypeStruct((nslots, BS, BS), jnp.bfloat16),
        in_specs=[smem] * 3 + [vmem] * 2 + [hbm] * 2,
        out_specs=hbm,
        scratch_shapes=[
            pltpu.VMEM((NP + 1, BS, BS), jnp.bfloat16),
            pltpu.VMEM((T, R, BS), jnp.bfloat16),
            pltpu.VMEM((T, BS, R), jnp.bfloat16),
            pltpu.VMEM((NP + 1, R, R), jnp.bfloat16),
            pltpu.VMEM((T // 2, R, 2 * BS), jnp.bfloat16),
            pltpu.VMEM((T // 2, R, 2 * BS), jnp.bfloat16),
            pltpu.VMEM((R, R), jnp.float32),
            pltpu.VMEM((NP, 1, R), jnp.float32),
            pltpu.VMEM((G, R, R), jnp.bfloat16),
            pltpu.VMEM((G, R, R), jnp.bfloat16),
            pltpu.VMEM((G, R, BS), jnp.bfloat16),
            pltpu.VMEM((G, R, BS), jnp.bfloat16),
            pltpu.SemaphoreType.DMA((T,)),
            pltpu.SemaphoreType.DMA,
            pltpu.SemaphoreType.DMA,
        ],
        compiler_params=pltpu.CompilerParams(vmem_limit_bytes=59 * 2**20),
        cost_estimate=pl.CostEstimate(flops=25 * 10**9, bytes_accessed=12 * 10**6, transcendentals=0),
        name="fock_pieces_direct" if direct else "fock_pieces",
    )(ids, slots, tables, core, coul, recv, factors)


CAP = 9
RELAY = 144
MESH = pl.DeviceIdType.MESH
ORDERS = ((2, 1, 0), (1, 0, 2), (0, 2, 1))


def line_of(u):
    chip = [(v * 43) >> 8 for v in u]
    col = [v - 6 * q for v, q in zip(u, chip)]
    e01 = chip[0] == chip[1]
    e02 = chip[0] == chip[2]
    e12 = chip[1] == chip[2]
    twice = e01 | e02 | e12
    over1 = e01
    over2 = e02 | e12
    where2 = jnp.where(e12, chip[1], chip[0])
    over_col = jnp.where(e01, col[1], col[2])
    third = jnp.where(e01, chip[2], jnp.where(e02, chip[1], chip[0]))
    rel = (third - where2) & 3
    return chip, col, twice, over1, over2, where2, over_col, rel


def route_kernel(place, ids, tab, idt, plus_s, minus_s, rankp_s, rankm_s):
    z, y, x, c = place[0], place[1], place[2], place[3]
    idt[...] = ids[...].astype(jnp.float32).T.astype(jnp.int32)
    lane = lax.broadcasted_iota(jnp.int32, (1, 128), 1)
    rows8 = lax.broadcasted_iota(jnp.int32, (8, 128), 0)
    lanes8 = lax.broadcasted_iota(jnp.int32, (8, 128), 1)
    f32 = jnp.float32
    below = (
        lax.broadcasted_iota(jnp.int32, (128, 128), 0) < lax.broadcasted_iota(jnp.int32, (128, 128), 1)
    ).astype(f32).astype(jnp.bfloat16)

    def prefix(m):
        return jnp.dot(m.astype(jnp.bfloat16), below, preferred_element_type=f32)

    lines = []
    fp, fm, fl = [], [], []
    for g in range(4):
        u = [idt[3 * g + j:3 * g + j + 1, :] - 24 * g for j in range(3)]
        ln = line_of(u)
        lines.append(ln)
        chip, col, twice, over1, over2, where2, over_col, rel = ln
        kind = jnp.where(twice, rel, 0)
        at = jnp.broadcast_to(where2, (8, 128)) == rows8 // 2
        here = at & ((lanes8 & 1) == (rows8 & 1))
        kind8 = jnp.broadcast_to(kind, (8, 128))
        fp.append(jnp.where(here & (kind8 == 3), 1.0, 0.0))
        fm.append(jnp.where(here & (kind8 == 1), 1.0, 0.0))
        fl.append(jnp.where(here & (kind8 == 2), 1.0, 0.0))
    fp = jnp.concatenate(fp, axis=0)
    fm = jnp.concatenate(fm, axis=0)
    fl = jnp.concatenate(fl, axis=0)
    np_ = jnp.sum(fp, axis=1, keepdims=True)
    nm_ = jnp.sum(fm, axis=1, keepdims=True)
    nl_ = jnp.sum(fl, axis=1, keepdims=True)
    give = jnp.clip(jnp.floor((nl_ + nm_ - np_ + 1.0) * 0.5), 0.0, nl_)
    first = fl * jnp.where(prefix(fl) < give, 1.0, 0.0)
    plus = fp + first
    minus = fm + fl - first
    plus_s[...] = plus
    minus_s[...] = minus
    rankp_s[...] = prefix(plus)
    rankm_s[...] = prefix(minus)
    most = jnp.max(jnp.maximum(jnp.sum(plus, axis=1, keepdims=True), jnp.sum(minus, axis=1, keepdims=True)), axis=0, keepdims=True)

    me = ((z * 4 + y) * 4 + x) * 2 + c
    own = jnp.zeros((1, 128), jnp.int32)
    for g in range(4):
        chip, col, twice, over1, over2, where2, over_col, rel = lines[g]
        goes = jnp.sum(plus[8 * g:8 * g + 8], axis=0, keepdims=True) > 0.5
        to = (where2 + jnp.where(goes, 1, 3)) & 3
        slots = [chip[0], jnp.where(over1, to, chip[1]), jnp.where(over2, to, chip[2])]
        for j in range(3):
            mine = jnp.sum(jnp.where(lane == me, slots[j], 0).astype(f32), axis=1, keepdims=True)
            own = own + jnp.where(lane == 3 * g + j, mine.astype(jnp.int32), 0)
    own = own + jnp.where(lane == 127, (most > CAP + 0.5).astype(jnp.int32), 0)

    u = [idt[pl.ds(3 * y + j, 1), :] - 24 * y for j in range(3)]
    chip, col, twice, over1, over2, where2, over_col, rel = line_of(u)
    rk = [idt[pl.ds(3 * z + k, 1), :] - 24 * z for k in range(3)]
    line_row = y * 8 + x * 2 + c
    left_row = y * 8 + ((x + 3) & 3) * 2 + c
    right_row = y * 8 + ((x + 1) & 3) * 2 + c

    def pool_col(v):
        core = jnp.where(v >= 3, 1, 0)
        return jnp.where(core == c, 0, 72) + v - 3 * core

    main = jnp.full((1, 128), -1, jnp.int32)
    for j, over in enumerate((chip[0] < 0, over1, over2)):
        main = jnp.where((chip[j] == x) & jnp.logical_not(over), pool_col(col[j]), main)
    from_left = plus_s[pl.ds(left_row, 1), :] > 0.5
    rank_left = rankp_s[pl.ds(left_row, 1), :].astype(jnp.int32)
    from_right = minus_s[pl.ds(right_row, 1), :] > 0.5
    rank_right = rankm_s[pl.ds(right_row, 1), :].astype(jnp.int32)
    for k in range(3):
        idx = jnp.where(main >= 0, main + rk[k] * 3, -1)
        idx = jnp.where(from_left, RELAY + rank_left, idx)
        idx = jnp.where(from_right, RELAY + CAP + rank_right, idx)
        tab[k:k + 1, :] = idx
    tab[3:7, :] = jnp.zeros((4, 128), jnp.int32)
    tab[7:8, :] = own

    j16 = lax.broadcasted_iota(jnp.int32, (16, 128), 0)
    l16 = lax.broadcasted_iota(jnp.int32, (16, 128), 1)
    out = jnp.zeros((16, 128), jnp.int32)

    def listed(flag, rank, value):
        sel = jnp.broadcast_to(flag, (16, 128)) & (jnp.broadcast_to(rank, (16, 128)) == j16)
        got = jnp.sum(jnp.where(sel, jnp.broadcast_to(value, (16, 128)) + 1, 0).astype(f32), axis=1, keepdims=True)
        return got.astype(jnp.int32) - 1

    my_plus = plus_s[pl.ds(line_row, 1), :] > 0.5
    my_rankp = rankp_s[pl.ds(line_row, 1), :].astype(jnp.int32)
    my_minus = minus_s[pl.ds(line_row, 1), :] > 0.5
    my_rankm = rankm_s[pl.ds(line_row, 1), :].astype(jnp.int32)
    for k in range(3):
        value = pool_col(over_col) + rk[k] * 3
        out = jnp.where(l16 == k, listed(my_plus, my_rankp, value), out)
        out = jnp.where(l16 == 3 + k, listed(my_minus, my_rankm, value), out)
    out = jnp.where(l16 == 6, listed(from_left, rank_left, lane), out)
    out = jnp.where(l16 == 7, listed(from_right, rank_right, lane), out)
    tab[8:24, :] = out


def route(place, ids):
    smem = pl.BlockSpec(memory_space=pltpu.SMEM)
    vmem = pl.BlockSpec(memory_space=pltpu.VMEM)
    return pl.pallas_call(
        route_kernel,
        out_shape=jax.ShapeDtypeStruct((24, 128), jnp.int32),
        in_specs=[smem, vmem],
        out_specs=vmem,
        scratch_shapes=[pltpu.VMEM((128, 128), jnp.int32)] + [pltpu.VMEM((32, 128), jnp.float32)] * 4,
        name="route_tasks",
    )(place, ids)


def here():
    z = lax.axis_index("row")
    b = lax.axis_index("bulk")
    return b // 2 % 4, b // 8, z, b % 2


def device(x, y, z, c):
    return (z, y * 8 + x * 2 + c)


def moved(at, axis, by):
    pos = list(at[:3])
    pos[axis] = lax.rem(pos[axis] + by, 4)
    return device(*pos, at[3])


def greet(at):
    barrier = pltpu.get_barrier_semaphore()
    for axis in range(3):
        for by in (1, 2, 3):
            pl.semaphore_signal(barrier, inc=1, device_id=moved(at, axis, by), device_id_type=MESH)
    pl.semaphore_wait(barrier, 9)


def part(ref, axis, index):
    if axis == 2:
        return ref.at[index]
    if axis == 1:
        return ref.at[:, index]
    return ref.at[:, :, index]


def phase_copies(at, k, step, src, dst, send, recv, local):
    axis = ORDERS[k][step]
    own = at[axis]
    copies = [pltpu.make_async_copy(part(src, axis, own), part(dst, axis, own), local.at[k, step])]
    for by in (1, 2, 3):
        to = lax.rem(own + by, 4)
        copies.append(
            pltpu.make_async_remote_copy(
                part(src, axis, to), part(dst, axis, own),
                send.at[k, step, by - 1], recv.at[k, step, by - 1],
                device_id=moved(at, axis, by), device_id_type=MESH,
            )
        )
    return copies


def start_all(copies):
    for copy in copies:
        copy.start()


def wait_all(copies):
    for copy in copies:
        copy.wait()


def share_kernel(mine, density, ids, sibling, buf, line, send, recv, swap_send, swap_recv):
    at = here()
    x, y, z, c = at
    barrier = pltpu.get_barrier_semaphore()
    for axis in range(3):
        for by in (1, 2, 3):
            pl.semaphore_signal(barrier, inc=1, device_id=moved(at, axis, by), device_id_type=MESH)
    pl.semaphore_signal(barrier, inc=1, device_id=device(x, y, z, 1 - c), device_id_type=MESH)
    line[...] = jnp.zeros_like(line)
    line[:, :T] = mine[...]
    buf[z, y, x, c] = line[...]
    pl.semaphore_wait(barrier, 10)
    swap = pltpu.make_async_remote_copy(
        density, sibling, swap_send, swap_recv, device_id=device(x, y, z, 1 - c), device_id_type=MESH
    )
    pair = pltpu.make_async_remote_copy(
        buf.at[z, y, x, c], buf.at[z, y, x, c], send.at[9], recv.at[9],
        device_id=device(x, y, z, 1 - c), device_id_type=MESH,
    )
    pair.start()
    pair.wait()
    swap.start()
    for axis, held in ((0, buf.at[z, y, x]), (1, buf.at[z, y]), (2, buf.at[z])):
        copies = [
            pltpu.make_async_remote_copy(
                held, held, send.at[3 * axis + by - 1], recv.at[3 * axis + by - 1],
                device_id=moved(at, axis, by), device_id_type=MESH,
            )
            for by in (1, 2, 3)
        ]
        start_all(copies)
        wait_all(copies)
    for d in range(128):
        ids[d:d + 1, :] = buf[d // 32, d // 8 % 4, d // 2 % 4, d % 2]
    swap.wait()


def share_tasks(mine, density):
    vmem = pl.BlockSpec(memory_space=pltpu.VMEM)
    hbm = pl.BlockSpec(memory_space=pl.ANY)
    dma = pltpu.SemaphoreType.DMA
    return pl.pallas_call(
        share_kernel,
        out_shape=[jax.ShapeDtypeStruct((128, 128), jnp.int32), jax.ShapeDtypeStruct((72, BS, BS), jnp.bfloat16)],
        in_specs=[vmem, hbm],
        out_specs=[vmem, hbm],
        scratch_shapes=[pltpu.VMEM((4, 4, 4, 2, 1, 128), jnp.int32), pltpu.VMEM((1, 128), jnp.int32)]
        + [dma((10,)), dma((10,)), dma, dma],
        compiler_params=pltpu.CompilerParams(collective_id=3, has_side_effects=True),
        name="share_tasks",
    )(mine, density.reshape(72, BS, BS))


def fetch_kernel(tab, density, sibling, out, pool, r0, r1, r2, rs, a, b, d,
                 load, relay_send, relay_recv, send, recv, local):
    at = here()
    c = at[3]
    mine = pltpu.make_async_copy(density, pool.at[pl.ds(0, 72)], load.at[0])
    other = pltpu.make_async_copy(sibling, pool.at[pl.ds(72, 72)], load.at[1])
    mine.start()
    other.start()
    greet(at)
    mine.wait()
    other.wait()
    relayed = (r0, r1, r2)
    relays = []
    for k in range(3):
        def fill(j, cc, k=k):
            rs[k, j] = pool[jnp.maximum(tab[8 + j, k], 0)]
            rs[k, CAP + j] = pool[jnp.maximum(tab[8 + j, 3 + k], 0)]
            return cc
        lax.fori_loop(0, CAP, fill, 0)
        pair = [
            pltpu.make_async_remote_copy(
                rs.at[k, pl.ds(CAP * side, CAP)], relayed[k].at[pl.ds(CAP * side, CAP)],
                relay_send.at[k, side], relay_recv.at[k, side],
                device_id=moved(at, 0, 1 if side == 0 else 3), device_id_type=MESH,
            )
            for side in range(2)
        ]
        start_all(pair)
        relays.append(pair)
    steps = []
    for k in range(3):
        wait_all(relays[k])

        def fill(i, cc, k=k):
            index = tab[k, 2 * i + c]
            plain = pool[jnp.clip(index, 0, 143)]
            passed = relayed[k][jnp.clip(index - RELAY, 0, 2 * CAP - 1)]
            a[k, i // 16, i // 4 % 4, i % 4] = jnp.where(index >= RELAY, passed, plain)
            return cc

        lax.fori_loop(0, 64, fill, 0)
        copies = phase_copies(at, k, 0, a.at[k], b.at[k], send, recv, local)
        start_all(copies)
        steps.append(copies)
    for step, src, dst in ((1, b, d), (2, d, out)):
        for k in range(3):
            wait_all(steps[k])
            copies = phase_copies(at, k, step, src.at[k], dst.at[k], send, recv, local)
            start_all(copies)
            steps[k] = copies
    for k in range(3):
        wait_all(steps[k])


def fetch_blocks(tab, density, sibling):
    smem = pl.BlockSpec(memory_space=pltpu.SMEM)
    hbm = pl.BlockSpec(memory_space=pl.ANY)
    cube = pltpu.VMEM((3, 4, 4, 4, BS, BS), jnp.bfloat16)
    dma = pltpu.SemaphoreType.DMA
    return pl.pallas_call(
        fetch_kernel,
        out_shape=jax.ShapeDtypeStruct((3, 4, 4, 4, BS, BS), jnp.bfloat16),
        in_specs=[smem, hbm, hbm],
        out_specs=hbm,
        scratch_shapes=[pltpu.VMEM((144, BS, BS), jnp.bfloat16)]
        + [pltpu.VMEM((2 * CAP, BS, BS), jnp.bfloat16)] * 3
        + [pltpu.VMEM((3, 2 * CAP, BS, BS), jnp.bfloat16), cube, cube, cube]
        + [dma((2,)), dma((3, 2)), dma((3, 2)), dma((3, 3, 3)), dma((3, 3, 3)), dma((3, 3))],
        compiler_params=pltpu.CompilerParams(
            collective_id=1, has_side_effects=True, vmem_limit_bytes=50 * 2**20
        ),
        name="fetch_blocks",
    )(tab, density.reshape(72, BS, BS), sibling.reshape(72, BS, BS))


def return_kernel(tab, pieces, out, back, b, d, e0, e1, e2, rs,
                  relay_send, relay_recv, send, recv, local, store):
    at = here()
    greet(at)
    ends = (e0, e1, e2)
    steps = []
    for k in range(3):
        copies = phase_copies(at, k, 0, pieces.at[k], b.at[k], send, recv, local)
        start_all(copies)
        steps.append(copies)
    for k in range(3):
        wait_all(steps[k])
        steps[k] = phase_copies(at, k, 1, b.at[k], d.at[k], send, recv, local)
        start_all(steps[k])
    for k in range(3):
        wait_all(steps[k])
        steps[k] = phase_copies(at, k, 2, d.at[k], ends[k], send, recv, local)
        start_all(steps[k])
    for k in range(3):
        wait_all(steps[k])
        kept = pltpu.make_async_copy(ends[k], out.at[k], store.at[k])
        kept.start()

        def fill(j, cc, k=k):
            for side in range(2):
                t = jnp.maximum(tab[8 + j, 6 + side], 0) // 2
                rs[k, side * CAP + j] = ends[k][t // 16, t // 4 % 4, t % 4]
            return cc

        lax.fori_loop(0, CAP, fill, 0)
        pair = [
            pltpu.make_async_remote_copy(
                rs.at[k, pl.ds(CAP * side, CAP)], back.at[k, pl.ds(CAP * side, CAP)],
                relay_send.at[k, side], relay_recv.at[k, side],
                device_id=moved(at, 0, 3 if side == 0 else 1), device_id_type=MESH,
            )
            for side in range(2)
        ]
        start_all(pair)
        steps[k] = pair + [kept]
    for k in range(3):
        wait_all(steps[k])


def return_pieces(tab, pieces):
    smem = pl.BlockSpec(memory_space=pltpu.SMEM)
    hbm = pl.BlockSpec(memory_space=pl.ANY)
    cube = pltpu.VMEM((3, 4, 4, 4, BS, BS), jnp.bfloat16)
    dma = pltpu.SemaphoreType.DMA
    return pl.pallas_call(
        return_kernel,
        out_shape=[
            jax.ShapeDtypeStruct((3, 4, 4, 4, BS, BS), jnp.bfloat16),
            jax.ShapeDtypeStruct((3, 2 * CAP, BS, BS), jnp.bfloat16),
        ],
        in_specs=[smem, hbm],
        out_specs=[hbm, hbm],
        scratch_shapes=[cube, cube]
        + [pltpu.VMEM((4, 4, 4, BS, BS), jnp.bfloat16)] * 3
        + [pltpu.VMEM((3, 2 * CAP, BS, BS), jnp.bfloat16)]
        + [dma((3, 2)), dma((3, 2)), dma((3, 3, 3)), dma((3, 3, 3)), dma((3, 3)), dma((3,))],
        compiler_params=pltpu.CompilerParams(
            collective_id=2, has_side_effects=True, vmem_limit_bytes=50 * 2**20
        ),
        name="return_pieces",
    )(tab, pieces)


def collect_kernel(half, place, tab, got, back, *rest):
    if half:
        out, total, got_v, back_v, sems = rest
    else:
        part, out, got_v, back_v, sems = rest
        total = out
    c = place[3]
    loads = []
    for k in range(3):
        loads.append(
            (
                pltpu.make_async_copy(got.at[k], got_v.at[k], sems.at[0, k]),
                pltpu.make_async_copy(back.at[k], back_v.at[k], sems.at[1, k]),
            )
        )
        start_all(loads[k])
    total[...] = jnp.zeros_like(total) if half else part[...].astype(jnp.float32)

    def put(index, block):
        index = index - 72 * half

        @pl.when((index >= 0) & (index < 72))
        def _():
            total[jnp.clip(index, 0, 71)] += block().astype(jnp.float32)

    for k in range(3):
        wait_all(loads[k])

        def add(i, cc, k=k):
            for n in range(4):
                put(tab[k, 8 * i + 2 * n + c], lambda: got_v[k, 4 * i + n])
            return cc

        lax.fori_loop(0, 16, add, 0)

        def add_back(j, cc, k=k):
            for side in range(2):
                put(tab[8 + j, 3 * side + k], lambda: back_v[k, side * CAP + j])
            return cc

        lax.fori_loop(0, CAP, add_back, 0)
    if half:
        out[...] = total[...].astype(jnp.bfloat16)


def collect(half, place, tab, got, back, *part):
    smem = pl.BlockSpec(memory_space=pltpu.SMEM)
    vmem = pl.BlockSpec(memory_space=pltpu.VMEM)
    hbm = pl.BlockSpec(memory_space=pl.ANY)
    return pl.pallas_call(
        functools.partial(collect_kernel, half),
        out_shape=jax.ShapeDtypeStruct((72, BS, BS), jnp.bfloat16 if half else jnp.float32),
        in_specs=[smem, smem, hbm, hbm] + [vmem] * len(part),
        out_specs=vmem,
        scratch_shapes=([pltpu.VMEM((72, BS, BS), jnp.float32)] if half else [])
        + [
            pltpu.VMEM((3, 64, BS, BS), jnp.bfloat16),
            pltpu.VMEM((3, 2 * CAP, BS, BS), jnp.bfloat16),
            pltpu.SemaphoreType.DMA((2, 3)),
        ],
        compiler_params=pltpu.CompilerParams(vmem_limit_bytes=50 * 2**20),
        name="collect_sibling" if half else "collect_own",
    )(place, tab, got.reshape(3, 64, BS, BS), back, *part)


def swap_cores(value):
    return lax.ppermute(value, "bulk", [(i, i ^ 1) for i in range(32)])


def fast_path(density, factors, core, mine, sibling, tables, place, tab, coul):
    recv = fetch_blocks(tab, density, sibling).reshape(192, BS, BS)
    pieces = compute(mine, tab, tables, core, coul, recv, factors, 192)
    got, back = return_pieces(tab, pieces.reshape(3, 4, 4, 4, BS, BS))
    part = swap_cores(collect(1, place, tab, got, back))
    return collect(0, place, tab, got, back, part).reshape(24, 3, BS, BS)


def column_of(ids, d, bulk):
    group = bulk // 8
    local = jnp.int32(-1)
    for j in range(3):
        block = ids[d * T + group * 3 + j]
        local = jnp.where(block // 3 == bulk, block % 3, local)
    return local


def pack_kernel(place, ids, density, out, sem):
    row = place[0]
    bulk = place[1]

    def copy(d, j, col):
        r = ids[d * T + row * 3 + j] - row * 24
        return pltpu.make_async_copy(density.at[r, col], out.at[d * 3 + j], sem)

    def send(d, n):
        col = column_of(ids, d, bulk)

        @pl.when(col >= 0)
        def _():
            for j in range(3):
                copy(d, j, col).start()

        return n + (col >= 0).astype(jnp.int32)

    n = lax.fori_loop(0, 128, send, 0)

    def drain(i, c):
        pltpu.make_async_copy(out.at[pl.ds(0, 3)], out.at[pl.ds(0, 3)], sem).wait()
        return c

    lax.fori_loop(0, n, drain, 0)


def pack(place, ids, density):
    smem = pl.BlockSpec(memory_space=pltpu.SMEM)
    hbm = pl.BlockSpec(memory_space=pl.ANY)
    return pl.pallas_call(
        pack_kernel,
        out_shape=jax.ShapeDtypeStruct((384, BS, BS), jnp.bfloat16),
        in_specs=[smem, smem, hbm],
        out_specs=hbm,
        scratch_shapes=[pltpu.SemaphoreType.DMA],
        name="pack_density",
    )(place, ids, density)


def gather_kernel(place, ids, inbound, fock, buf, sems):
    row = place[0]
    bulk = place[1]

    def fetch(d, c):
        @pl.when(column_of(ids, d, bulk) >= 0)
        def _():
            pltpu.make_async_copy(inbound.at[pl.ds(d * 3, 3)], buf.at[pl.ds(d * 3, 3)], sems.at[d]).start()

        return c

    lax.fori_loop(0, 128, fetch, 0)
    fock[...] = jnp.zeros_like(fock)

    def add(d, c):
        col = column_of(ids, d, bulk)

        @pl.when(col >= 0)
        def _():
            pltpu.make_async_copy(inbound.at[pl.ds(d * 3, 3)], buf.at[pl.ds(d * 3, 3)], sems.at[d]).wait()
            for j in range(3):
                r = ids[d * T + row * 3 + j] - row * 24
                fock[r, col] += buf[d * 3 + j].astype(jnp.float32)

        return c

    lax.fori_loop(0, 128, add, 0)


def gather(place, ids, inbound):
    smem = pl.BlockSpec(memory_space=pltpu.SMEM)
    vmem = pl.BlockSpec(memory_space=pltpu.VMEM)
    hbm = pl.BlockSpec(memory_space=pl.ANY)
    return pl.pallas_call(
        gather_kernel,
        out_shape=jax.ShapeDtypeStruct((24, 3, BS, BS), jnp.float32),
        in_specs=[smem, smem, hbm],
        out_specs=vmem,
        scratch_shapes=[pltpu.VMEM((384, BS, BS), jnp.bfloat16), pltpu.SemaphoreType.DMA((128,))],
        compiler_params=pltpu.CompilerParams(vmem_limit_bytes=40 * 2**20),
        name="add_pieces",
    )(place, ids, inbound)


def slow_path(density, factors, core, mine, tables, place, tab, ids, coul):
    axes = ("row", "bulk")
    where = jnp.stack([place[0], place[1] * 8 + place[2] * 2 + place[3]])
    ids = ids[:, :T].reshape(-1)
    sent = pack(where, ids, density)
    recv = lax.all_to_all(sent, axes, split_axis=0, concat_axis=0, tiled=True)
    owner = mine[:, None] // 24 * 32 + mine[None, :] // 3
    slot = (owner * 3 + (jnp.arange(T) % 3)[:, None]).reshape(-1)
    pieces = compute(mine, tab, tables, core, coul, recv[slot], factors, NP, direct=True)
    outbound = jnp.zeros((384, BS, BS), jnp.bfloat16).at[slot].set(pieces)
    inbound = lax.all_to_all(outbound, axes, split_axis=0, concat_axis=0, tiled=True)
    return gather(where, ids, inbound)


def shards(density, factors, core, task_blocks, quartets, quartet_count):
    mine = task_blocks[0]
    bulk = lax.axis_index("bulk")
    place = jnp.stack([lax.axis_index("row"), bulk // 8, bulk // 2 % 4, bulk % 2]).astype(jnp.int32)
    ids, sibling = share_tasks(task_blocks, density)
    tables, coul = entries(quartets, quartet_count)
    tab = route(place, ids)
    fock = fast_path(density, factors, core, mine, sibling, tables, place, tab, coul)

    def again(state):
        return state[0]

    def padded(state):
        return jnp.array(False), slow_path(density, factors, core, mine, tables, place, tab, ids, coul)

    return lax.while_loop(again, padded, (tab[7, 127] > 0, fock))[1]


def solution(mesh):
    return jax.shard_map(
        shards,
        mesh=mesh,
        in_specs=(
            P("row", "bulk", None, None),
            P(),
            P(),
            P(("row", "bulk"), None),
            P(("row", "bulk"), None),
            P(("row", "bulk")),
        ),
        out_specs=P("row", "bulk", None, None),
        check_vma=False,
    )
```

```python
import functools

import jax
import jax.numpy as jnp
from jax import lax
from jax.experimental import pallas as pl
from jax.experimental.pallas import tpu as pltpu
from jax.sharding import PartitionSpec as P

T = 12
NP = 144
R = 384
BS = 128
CAPE = 512
G = 4
LEVELS = 7
STRIP = 64


def entries_kernel(quads, count, tables, coul):
    f32 = jnp.float32
    live = lax.broadcasted_iota(jnp.int32, (128, 1), 0) < count[0]
    q = jnp.concatenate([quads[...], jnp.zeros((4, 128), jnp.int32)], axis=0).astype(f32).T.astype(jnp.int32)
    a, b, c, e = (q[:, n:n + 1] for n in range(4))
    lanes = lax.broadcasted_iota(jnp.int32, (128, 256), 1)

    def hot(t):
        return jnp.where((t == lanes) & live, 1.0, 0.0)

    def product(u, v):
        return jnp.dot(u.T.astype(jnp.bfloat16), v.astype(jnp.bfloat16), preferred_element_type=f32)

    bra = hot(a * T + b)
    ket = hot(c * T + e)
    table = 2.0 * (product(bra, ket) + product(ket, bra))
    coul[...] = table[:NP, :NP]

    targets = [a * T + c, a * T + e, b * T + c, b * T + e]
    sources = [b * T + e, b * T + c, a * T + e, a * T + c]
    member = jnp.concatenate([hot(t) for t in targets], axis=0)
    source = jnp.concatenate(sources, axis=0).astype(f32)
    older = lax.broadcasted_iota(jnp.int32, (CAPE, CAPE), 0) > lax.broadcasted_iota(jnp.int32, (CAPE, CAPE), 1)
    rank = jnp.dot(
        jnp.where(older, 1.0, 0.0).astype(jnp.bfloat16), member.astype(jnp.bfloat16), preferred_element_type=f32
    )
    counts = jnp.broadcast_to(jnp.sum(member, axis=0, keepdims=True), (8, 256))
    row = lax.broadcasted_iota(jnp.int32, (256, 256), 0)
    col = lax.broadcasted_iota(jnp.int32, (256, 256), 1)
    start = jnp.dot(
        counts, jnp.where(row < col, 1.0, 0.0), precision=lax.Precision.HIGHEST, preferred_element_type=f32
    )
    used = jnp.sum(member, axis=1, keepdims=True) > 0.5
    place = jnp.sum(member * (rank + start[0:1]), axis=1, keepdims=True)
    place = jnp.where(used, place, -1.0).astype(jnp.int32)
    spots = lax.broadcasted_iota(jnp.int32, (CAPE, CAPE + 128), 1)
    filled = jnp.sum(jnp.where(place == spots, source - NP, 0.0), axis=0, keepdims=True)

    level = jnp.minimum(counts, LEVELS + 1.0)
    level = jnp.where(lax.broadcasted_iota(jnp.int32, (8, 256), 1) < NP, level, -1.0)
    across = jnp.broadcast_to(level[0:1], (256, 256))
    down = across.T
    ahead = (across > down) | ((across == down) & (col < row))
    spot = jnp.sum(jnp.where(ahead, 1.0, 0.0), axis=1, keepdims=True).astype(jnp.int32)
    order = jnp.sum(jnp.where(spot == col, row, 0).astype(f32), axis=0, keepdims=True)
    order = jnp.minimum(order, float(NP))
    tables[0:1, :] = (filled + NP).astype(jnp.int32)
    tables[1:2, 0:256] = start[0:1].astype(jnp.int32)
    tables[2:3, 0:256] = order.astype(jnp.int32)


def entries(quads, count):
    smem = pl.BlockSpec(memory_space=pltpu.SMEM)
    vmem = pl.BlockSpec(memory_space=pltpu.VMEM)
    return pl.pallas_call(
        entries_kernel,
        out_shape=[
            jax.ShapeDtypeStruct((8, CAPE + 128), jnp.int32),
            jax.ShapeDtypeStruct((NP, NP), jnp.float32),
        ],
        in_specs=[vmem, smem],
        out_specs=[vmem, vmem],
        cost_estimate=pl.CostEstimate(flops=10000, bytes_accessed=10000, transcendentals=0),
        name="sort_entries",
    )(quads.T, count)


def split(t):
    x = (t * 171) >> 11
    return x, t - x * T


def slot_of(direct, slots, t):
    if direct:
        return t
    x, y = split(t)
    z = (x * 11) >> 5
    return (x - 3 * z) * 64 + z * 16 + ((y * 11) >> 5) * 4 + slots[7, y]


def compute_kernel(direct, ids, slots, tables, core, coul, recv, factors, outbound,
                   dens, fac, fact, pw, ha, hb, corem, pot, cma, cmb, rha, rhb, in_sem, fac_sem, out_sem):
    for x in range(T):
        pltpu.make_async_copy(factors.at[ids[x]], fac.at[x], fac_sem).start()
    for x in range(T):
        def fetch(y, c, x=x):
            pltpu.make_async_copy(recv.at[slot_of(direct, slots, x * T + y)], dens.at[x * T + y], in_sem.at[x]).start()
            return c
        lax.fori_loop(0, T, fetch, 0)
    corem[...] = core[...] * -0.5
    pw[NP] = jnp.zeros((R, R), jnp.bfloat16)
    pltpu.make_async_copy(factors.at[pl.ds(0, T)], fac, fac_sem).wait()
    for x in range(T):
        fact[x] = fac[x].T

    eye = lax.broadcasted_iota(jnp.int32, (BS, BS), 0) == lax.broadcasted_iota(jnp.int32, (BS, BS), 1)

    def halves(x, hs):
        pltpu.make_async_copy(recv.at[pl.ds(0, T)], dens.at[pl.ds(0, T)], in_sem.at[x]).wait()
        fx = fac[x]
        for yp in range(T // 2):
            s = x * T + 2 * yp
            d2 = jnp.concatenate([dens[s], dens[s + 1]], axis=1)
            hs[yp] = jnp.dot(fx, d2, preferred_element_type=jnp.float32).astype(jnp.bfloat16)

    def pairs_of(x, hs):
        for y in range(T):
            s = x * T + y
            h = hs[y // 2, :, (y % 2) * BS:(y % 2 + 1) * BS]
            p = jnp.dot(h, fact[y], preferred_element_type=jnp.float32)
            pw[s] = p.astype(jnp.bfloat16)
            dia = [
                jnp.sum(jnp.where(eye, p[k * BS:(k + 1) * BS, k * BS:(k + 1) * BS], 0.0), axis=0, keepdims=True)
                for k in range(3)
            ]
            pot[s] = jnp.concatenate(dia, axis=1)

    halves(0, ha)

    def both(k, c):
        halves(2 * k + 1, hb)
        pairs_of(2 * k, ha)
        halves(2 * k + 2, ha)
        pairs_of(2 * k + 1, hb)
        return c

    lax.fori_loop(0, T // 2 - 1, both, 0)
    halves(T - 1, hb)
    pairs_of(T - 2, ha)
    pairs_of(T - 1, hb)
    pair_diag = pot[...].reshape(NP, R)
    total = jnp.dot(coul[...], pair_diag, precision=lax.Precision.HIGHEST, preferred_element_type=jnp.float32)
    pot[...] = jnp.dot(total, core[...], precision=lax.Precision.HIGHEST, preferred_element_type=jnp.float32).reshape(NP, 1, R)

    def source(lo, n, e):
        return jnp.where(e < n, tables[0, lo + e], NP)

    def entry(lo, n, e, rows):
        return pw[source(lo, n, e), rows].astype(jnp.float32)

    def entries_at(lo, n, e, many, rows):
        one = pw[source(lo, n, e), rows]
        if many == 2:
            one = one + pw[source(lo, n, e + 1), rows]
        return one.astype(jnp.float32)

    def put_core_matrices(ts, cms, count, extra, rows):
        r = rows.start
        block = r // BS
        at = r % BS
        weight = corem[rows]
        mask = eye[at:at + STRIP]
        for q, t in enumerate(ts):
            lo = tables[1, t]
            n = tables[1, t + 1] - lo
            dia = jnp.where(mask, pot[t, :, block * BS:(block + 1) * BS], 0.0)
            cols3 = [jnp.zeros((STRIP, BS), jnp.float32)] * 3
            if count:
                es = entries_at(lo, n, 0, min(2, count), rows)
                for k in range(2, count, 2):
                    es = es + entries_at(lo, n, k, min(2, count - k), rows)
                if extra:
                    es = lax.fori_loop(count, n, lambda k, v: v + entry(lo, n, k, rows), es)
                cm = weight * es
                cols3 = [cm[:, j * BS:(j + 1) * BS] for j in range(3)]
            cols3[block] = cols3[block] + dia
            cms[q, rows] = jnp.concatenate(cols3, axis=1).astype(jnp.bfloat16)

    def step(i, cm_now, cm_before, rh_now, rh_before):

        def ranked(j):
            return jnp.where(j >= 0, tables[2, jnp.maximum(j, 0)], NP)

        tg = [ranked(i * G + q) for q in range(G)]
        t1 = [ranked((i - 1) * G + q) for q in range(G)]
        t2 = [ranked((i - 2) * G + q) for q in range(G)]

        def late(q):
            x2, _ = split(jnp.minimum(t2[q], NP - 1))
            _, y1 = split(t1[q])
            dens[t2[q]] = jnp.dot(fact[x2], rh_before[q], preferred_element_type=jnp.float32).astype(jnp.bfloat16)
            rh_now[q] = jnp.dot(
                cm_before[q], fac[y1], preferred_element_type=jnp.float32
            ).astype(jnp.bfloat16)

        def branch(count, extra):
            def run():
                strips = R // STRIP
                for part in range(strips):
                    for q in range(part * G // strips, (part + 1) * G // strips):
                        late(q)
                    if count is not None:
                        put_core_matrices(tg, cm_now, count, extra, slice(part * STRIP, (part + 1) * STRIP))
            return run

        top = tables[1, tg[0] + 1] - tables[1, tg[0]]
        top = jnp.where(i < NP // G, top, -1)
        lax.switch(
            jnp.minimum(top, LEVELS + 1) + 1,
            [branch(None, False)] + [branch(k, False) for k in range(LEVELS + 1)] + [branch(LEVELS, True)],
        )
        @pl.when(i >= 2)
        def _():
            for q in range(G):
                pltpu.make_async_copy(dens.at[t2[q]], outbound.at[slot_of(direct, slots, t2[q])], out_sem).start()

    def steps(k, c):
        step(2 * k, cma, cmb, rha, rhb)
        step(2 * k + 1, cmb, cma, rhb, rha)
        return c

    lax.fori_loop(0, (NP // G + 2) // 2, steps, 0)
    pltpu.make_async_copy(dens.at[pl.ds(0, NP)], outbound.at[pl.ds(0, NP)], out_sem).wait()


def compute(ids, slots, tables, core, coul, recv, factors, nslots, direct=False):
    smem = pl.BlockSpec(memory_space=pltpu.SMEM)
    vmem = pl.BlockSpec(memory_space=pltpu.VMEM)
    hbm = pl.BlockSpec(memory_space=pl.ANY)
    return pl.pallas_call(
        functools.partial(compute_kernel, direct),
        out_shape=jax.ShapeDtypeStruct((nslots, BS, BS), jnp.bfloat16),
        in_specs=[smem] * 3 + [vmem] * 2 + [hbm] * 2,
        out_specs=hbm,
        scratch_shapes=[
            pltpu.VMEM((NP + 1, BS, BS), jnp.bfloat16),
            pltpu.VMEM((T, R, BS), jnp.bfloat16),
            pltpu.VMEM((T, BS, R), jnp.bfloat16),
            pltpu.VMEM((NP + 1, R, R), jnp.bfloat16),
            pltpu.VMEM((T // 2, R, 2 * BS), jnp.bfloat16),
            pltpu.VMEM((T // 2, R, 2 * BS), jnp.bfloat16),
            pltpu.VMEM((R, R), jnp.float32),
            pltpu.VMEM((NP, 1, R), jnp.float32),
            pltpu.VMEM((G, R, R), jnp.bfloat16),
            pltpu.VMEM((G, R, R), jnp.bfloat16),
            pltpu.VMEM((G, R, BS), jnp.bfloat16),
            pltpu.VMEM((G, R, BS), jnp.bfloat16),
            pltpu.SemaphoreType.DMA((T,)),
            pltpu.SemaphoreType.DMA,
            pltpu.SemaphoreType.DMA,
        ],
        compiler_params=pltpu.CompilerParams(vmem_limit_bytes=59 * 2**20),
        cost_estimate=pl.CostEstimate(flops=25 * 10**9, bytes_accessed=12 * 10**6, transcendentals=0),
        name="fock_pieces_direct" if direct else "fock_pieces",
    )(ids, slots, tables, core, coul, recv, factors)


CAP = 9
RELAY = 144
MESH = pl.DeviceIdType.MESH
ORDERS = ((2, 1, 0), (1, 0, 2), (0, 2, 1))


def line_of(u):
    chip = [(v * 43) >> 8 for v in u]
    col = [v - 6 * q for v, q in zip(u, chip)]
    e01 = chip[0] == chip[1]
    e02 = chip[0] == chip[2]
    e12 = chip[1] == chip[2]
    twice = e01 | e02 | e12
    over1 = e01
    over2 = e02 | e12
    where2 = jnp.where(e12, chip[1], chip[0])
    over_col = jnp.where(e01, col[1], col[2])
    third = jnp.where(e01, chip[2], jnp.where(e02, chip[1], chip[0]))
    rel = (third - where2) & 3
    return chip, col, twice, over1, over2, where2, over_col, rel


def route_kernel(place, ids, tab, idt, plus_s, minus_s, rankp_s, rankm_s):
    z, y, x, c = place[0], place[1], place[2], place[3]
    idt[...] = ids[...].astype(jnp.float32).T.astype(jnp.int32)
    lane = lax.broadcasted_iota(jnp.int32, (1, 128), 1)
    rows8 = lax.broadcasted_iota(jnp.int32, (8, 128), 0)
    lanes8 = lax.broadcasted_iota(jnp.int32, (8, 128), 1)
    f32 = jnp.float32
    below = (
        lax.broadcasted_iota(jnp.int32, (128, 128), 0) < lax.broadcasted_iota(jnp.int32, (128, 128), 1)
    ).astype(f32).astype(jnp.bfloat16)

    def prefix(m):
        return jnp.dot(m.astype(jnp.bfloat16), below, preferred_element_type=f32)

    lines = []
    fp, fm, fl = [], [], []
    for g in range(4):
        u = [idt[3 * g + j:3 * g + j + 1, :] - 24 * g for j in range(3)]
        ln = line_of(u)
        lines.append(ln)
        chip, col, twice, over1, over2, where2, over_col, rel = ln
        kind = jnp.where(twice, rel, 0)
        at = jnp.broadcast_to(where2, (8, 128)) == rows8 // 2
        here = at & ((lanes8 & 1) == (rows8 & 1))
        kind8 = jnp.broadcast_to(kind, (8, 128))
        fp.append(jnp.where(here & (kind8 == 3), 1.0, 0.0))
        fm.append(jnp.where(here & (kind8 == 1), 1.0, 0.0))
        fl.append(jnp.where(here & (kind8 == 2), 1.0, 0.0))
    fp = jnp.concatenate(fp, axis=0)
    fm = jnp.concatenate(fm, axis=0)
    fl = jnp.concatenate(fl, axis=0)
    np_ = jnp.sum(fp, axis=1, keepdims=True)
    nm_ = jnp.sum(fm, axis=1, keepdims=True)
    nl_ = jnp.sum(fl, axis=1, keepdims=True)
    give = jnp.clip(jnp.floor((nl_ + nm_ - np_ + 1.0) * 0.5), 0.0, nl_)
    first = fl * jnp.where(prefix(fl) < give, 1.0, 0.0)
    plus = fp + first
    minus = fm + fl - first
    plus_s[...] = plus
    minus_s[...] = minus
    rankp_s[...] = prefix(plus)
    rankm_s[...] = prefix(minus)
    most = jnp.max(jnp.maximum(jnp.sum(plus, axis=1, keepdims=True), jnp.sum(minus, axis=1, keepdims=True)), axis=0, keepdims=True)

    me = ((z * 4 + y) * 4 + x) * 2 + c
    own = jnp.zeros((1, 128), jnp.int32)
    for g in range(4):
        chip, col, twice, over1, over2, where2, over_col, rel = lines[g]
        goes = jnp.sum(plus[8 * g:8 * g + 8], axis=0, keepdims=True) > 0.5
        to = (where2 + jnp.where(goes, 1, 3)) & 3
        slots = [chip[0], jnp.where(over1, to, chip[1]), jnp.where(over2, to, chip[2])]
        for j in range(3):
            mine = jnp.sum(jnp.where(lane == me, slots[j], 0).astype(f32), axis=1, keepdims=True)
            own = own + jnp.where(lane == 3 * g + j, mine.astype(jnp.int32), 0)
    own = own + jnp.where(lane == 127, (most > CAP + 0.5).astype(jnp.int32), 0)

    u = [idt[pl.ds(3 * y + j, 1), :] - 24 * y for j in range(3)]
    chip, col, twice, over1, over2, where2, over_col, rel = line_of(u)
    rk = [idt[pl.ds(3 * z + k, 1), :] - 24 * z for k in range(3)]
    line_row = y * 8 + x * 2 + c
    left_row = y * 8 + ((x + 3) & 3) * 2 + c
    right_row = y * 8 + ((x + 1) & 3) * 2 + c

    def pool_col(v):
        core = jnp.where(v >= 3, 1, 0)
        return jnp.where(core == c, 0, 72) + v - 3 * core

    main = jnp.full((1, 128), -1, jnp.int32)
    for j, over in enumerate((chip[0] < 0, over1, over2)):
        main = jnp.where((chip[j] == x) & jnp.logical_not(over), pool_col(col[j]), main)
    from_left = plus_s[pl.ds(left_row, 1), :] > 0.5
    rank_left = rankp_s[pl.ds(left_row, 1), :].astype(jnp.int32)
    from_right = minus_s[pl.ds(right_row, 1), :] > 0.5
    rank_right = rankm_s[pl.ds(right_row, 1), :].astype(jnp.int32)
    for k in range(3):
        idx = jnp.where(main >= 0, main + rk[k] * 3, -1)
        idx = jnp.where(from_left, RELAY + rank_left, idx)
        idx = jnp.where(from_right, RELAY + CAP + rank_right, idx)
        tab[k:k + 1, :] = idx
    tab[3:7, :] = jnp.zeros((4, 128), jnp.int32)
    tab[7:8, :] = own

    j16 = lax.broadcasted_iota(jnp.int32, (16, 128), 0)
    l16 = lax.broadcasted_iota(jnp.int32, (16, 128), 1)
    out = jnp.zeros((16, 128), jnp.int32)

    def listed(flag, rank, value):
        sel = jnp.broadcast_to(flag, (16, 128)) & (jnp.broadcast_to(rank, (16, 128)) == j16)
        got = jnp.sum(jnp.where(sel, jnp.broadcast_to(value, (16, 128)) + 1, 0).astype(f32), axis=1, keepdims=True)
        return got.astype(jnp.int32) - 1

    my_plus = plus_s[pl.ds(line_row, 1), :] > 0.5
    my_rankp = rankp_s[pl.ds(line_row, 1), :].astype(jnp.int32)
    my_minus = minus_s[pl.ds(line_row, 1), :] > 0.5
    my_rankm = rankm_s[pl.ds(line_row, 1), :].astype(jnp.int32)
    for k in range(3):
        value = pool_col(over_col) + rk[k] * 3
        out = jnp.where(l16 == k, listed(my_plus, my_rankp, value), out)
        out = jnp.where(l16 == 3 + k, listed(my_minus, my_rankm, value), out)
    out = jnp.where(l16 == 6, listed(from_left, rank_left, lane), out)
    out = jnp.where(l16 == 7, listed(from_right, rank_right, lane), out)
    tab[8:24, :] = out


def route(place, ids):
    smem = pl.BlockSpec(memory_space=pltpu.SMEM)
    vmem = pl.BlockSpec(memory_space=pltpu.VMEM)
    return pl.pallas_call(
        route_kernel,
        out_shape=jax.ShapeDtypeStruct((24, 128), jnp.int32),
        in_specs=[smem, vmem],
        out_specs=vmem,
        scratch_shapes=[pltpu.VMEM((128, 128), jnp.int32)] + [pltpu.VMEM((32, 128), jnp.float32)] * 4,
        name="route_tasks",
    )(place, ids)


def here():
    z = lax.axis_index("row")
    b = lax.axis_index("bulk")
    return b // 2 % 4, b // 8, z, b % 2


def device(x, y, z, c):
    return (z, y * 8 + x * 2 + c)


def moved(at, axis, by):
    pos = list(at[:3])
    pos[axis] = lax.rem(pos[axis] + by, 4)
    return device(*pos, at[3])


def greet(at):
    barrier = pltpu.get_barrier_semaphore()
    for axis in range(3):
        for by in (1, 2, 3):
            pl.semaphore_signal(barrier, inc=1, device_id=moved(at, axis, by), device_id_type=MESH)
    pl.semaphore_wait(barrier, 9)


def part(ref, axis, index):
    if axis == 2:
        return ref.at[index]
    if axis == 1:
        return ref.at[:, index]
    return ref.at[:, :, index]


def phase_copies(at, k, step, src, dst, send, recv, local):
    axis = ORDERS[k][step]
    own = at[axis]
    copies = [pltpu.make_async_copy(part(src, axis, own), part(dst, axis, own), local.at[k, step])]
    for by in (1, 2, 3):
        to = lax.rem(own + by, 4)
        copies.append(
            pltpu.make_async_remote_copy(
                part(src, axis, to), part(dst, axis, own),
                send.at[k, step, by - 1], recv.at[k, step, by - 1],
                device_id=moved(at, axis, by), device_id_type=MESH,
            )
        )
    return copies


def start_all(copies):
    for copy in copies:
        copy.start()


def wait_all(copies):
    for copy in copies:
        copy.wait()


def share_kernel(mine, density, ids, sibling, buf, line, send, recv, swap_send, swap_recv):
    at = here()
    x, y, z, c = at
    barrier = pltpu.get_barrier_semaphore()
    for axis in range(3):
        for by in (1, 2, 3):
            pl.semaphore_signal(barrier, inc=1, device_id=moved(at, axis, by), device_id_type=MESH)
    pl.semaphore_signal(barrier, inc=1, device_id=device(x, y, z, 1 - c), device_id_type=MESH)
    line[...] = jnp.zeros_like(line)
    line[:, :T] = mine[...]
    buf[c, z, y, x] = line[...]
    pl.semaphore_wait(barrier, 10)
    swap = pltpu.make_async_remote_copy(
        density, sibling, swap_send, swap_recv, device_id=device(x, y, z, 1 - c), device_id_type=MESH
    )
    swap.start()
    for axis, held in ((0, buf.at[c, z, y, x]), (1, buf.at[c, z, y]), (2, buf.at[c, z])):
        copies = [
            pltpu.make_async_remote_copy(
                held, held, send.at[3 * axis + by - 1], recv.at[3 * axis + by - 1],
                device_id=moved(at, axis, by), device_id_type=MESH,
            )
            for by in (1, 2, 3)
        ]
        start_all(copies)
        wait_all(copies)
    pair = pltpu.make_async_remote_copy(
        buf.at[c], buf.at[c], send.at[9], recv.at[9],
        device_id=device(x, y, z, 1 - c), device_id_type=MESH,
    )
    pair.start()
    pair.wait()
    for d in range(128):
        ids[d:d + 1, :] = buf[d % 2, d // 32, d // 8 % 4, d // 2 % 4]
    swap.wait()


def share_tasks(mine, density):
    vmem = pl.BlockSpec(memory_space=pltpu.VMEM)
    hbm = pl.BlockSpec(memory_space=pl.ANY)
    dma = pltpu.SemaphoreType.DMA
    return pl.pallas_call(
        share_kernel,
        out_shape=[jax.ShapeDtypeStruct((128, 128), jnp.int32), jax.ShapeDtypeStruct((72, BS, BS), jnp.bfloat16)],
        in_specs=[vmem, hbm],
        out_specs=[vmem, hbm],
        scratch_shapes=[pltpu.VMEM((2, 4, 4, 4, 1, 128), jnp.int32), pltpu.VMEM((1, 128), jnp.int32)]
        + [dma((10,)), dma((10,)), dma, dma],
        compiler_params=pltpu.CompilerParams(collective_id=3, has_side_effects=True),
        name="share_tasks",
    )(mine, density.reshape(72, BS, BS))


def fetch_kernel(tab, density, sibling, out, pool, r0, r1, r2, rs, a, b, d,
                 load, relay_send, relay_recv, send, recv, local):
    at = here()
    c = at[3]
    mine = pltpu.make_async_copy(density, pool.at[pl.ds(0, 72)], load.at[0])
    other = pltpu.make_async_copy(sibling, pool.at[pl.ds(72, 72)], load.at[1])
    mine.start()
    other.start()
    greet(at)
    mine.wait()
    other.wait()
    relayed = (r0, r1, r2)
    relays = []
    for k in range(3):
        def fill(j, cc, k=k):
            rs[k, j] = pool[jnp.maximum(tab[8 + j, k], 0)]
            rs[k, CAP + j] = pool[jnp.maximum(tab[8 + j, 3 + k], 0)]
            return cc
        lax.fori_loop(0, CAP, fill, 0)
        pair = [
            pltpu.make_async_remote_copy(
                rs.at[k, pl.ds(CAP * side, CAP)], relayed[k].at[pl.ds(CAP * side, CAP)],
                relay_send.at[k, side], relay_recv.at[k, side],
                device_id=moved(at, 0, 1 if side == 0 else 3), device_id_type=MESH,
            )
            for side in range(2)
        ]
        start_all(pair)
        relays.append(pair)
    steps = []
    for k in range(3):
        wait_all(relays[k])

        def fill(i, cc, k=k):
            index = tab[k, 2 * i + c]
            plain = pool[jnp.clip(index, 0, 143)]
            passed = relayed[k][jnp.clip(index - RELAY, 0, 2 * CAP - 1)]
            a[k, i // 16, i // 4 % 4, i % 4] = jnp.where(index >= RELAY, passed, plain)
            return cc

        lax.fori_loop(0, 64, fill, 0)
        copies = phase_copies(at, k, 0, a.at[k], b.at[k], send, recv, local)
        start_all(copies)
        steps.append(copies)
    for step, src, dst in ((1, b, d), (2, d, out)):
        for k in range(3):
            wait_all(steps[k])
            copies = phase_copies(at, k, step, src.at[k], dst.at[k], send, recv, local)
            start_all(copies)
            steps[k] = copies
    for k in range(3):
        wait_all(steps[k])


def fetch_blocks(tab, density, sibling):
    smem = pl.BlockSpec(memory_space=pltpu.SMEM)
    hbm = pl.BlockSpec(memory_space=pl.ANY)
    cube = pltpu.VMEM((3, 4, 4, 4, BS, BS), jnp.bfloat16)
    dma = pltpu.SemaphoreType.DMA
    return pl.pallas_call(
        fetch_kernel,
        out_shape=jax.ShapeDtypeStruct((3, 4, 4, 4, BS, BS), jnp.bfloat16),
        in_specs=[smem, hbm, hbm],
        out_specs=hbm,
        scratch_shapes=[pltpu.VMEM((144, BS, BS), jnp.bfloat16)]
        + [pltpu.VMEM((2 * CAP, BS, BS), jnp.bfloat16)] * 3
        + [pltpu.VMEM((3, 2 * CAP, BS, BS), jnp.bfloat16), cube, cube, cube]
        + [dma((2,)), dma((3, 2)), dma((3, 2)), dma((3, 3, 3)), dma((3, 3, 3)), dma((3, 3))],
        compiler_params=pltpu.CompilerParams(
            collective_id=1, has_side_effects=True, vmem_limit_bytes=50 * 2**20
        ),
        name="fetch_blocks",
    )(tab, density.reshape(72, BS, BS), sibling.reshape(72, BS, BS))


def return_kernel(tab, pieces, out, back, b, d, e0, e1, e2, rs,
                  relay_send, relay_recv, send, recv, local, store):
    at = here()
    greet(at)
    ends = (e0, e1, e2)
    steps = []
    for k in range(3):
        copies = phase_copies(at, k, 0, pieces.at[k], b.at[k], send, recv, local)
        start_all(copies)
        steps.append(copies)
    for k in range(3):
        wait_all(steps[k])
        steps[k] = phase_copies(at, k, 1, b.at[k], d.at[k], send, recv, local)
        start_all(steps[k])
    for k in range(3):
        wait_all(steps[k])
        steps[k] = phase_copies(at, k, 2, d.at[k], ends[k], send, recv, local)
        start_all(steps[k])
    for k in range(3):
        wait_all(steps[k])
        kept = pltpu.make_async_copy(ends[k], out.at[k], store.at[k])
        kept.start()

        def fill(j, cc, k=k):
            for side in range(2):
                t = jnp.maximum(tab[8 + j, 6 + side], 0) // 2
                rs[k, side * CAP + j] = ends[k][t // 16, t // 4 % 4, t % 4]
            return cc

        lax.fori_loop(0, CAP, fill, 0)
        pair = [
            pltpu.make_async_remote_copy(
                rs.at[k, pl.ds(CAP * side, CAP)], back.at[k, pl.ds(CAP * side, CAP)],
                relay_send.at[k, side], relay_recv.at[k, side],
                device_id=moved(at, 0, 3 if side == 0 else 1), device_id_type=MESH,
            )
            for side in range(2)
        ]
        start_all(pair)
        steps[k] = pair + [kept]
    for k in range(3):
        wait_all(steps[k])


def return_pieces(tab, pieces):
    smem = pl.BlockSpec(memory_space=pltpu.SMEM)
    hbm = pl.BlockSpec(memory_space=pl.ANY)
    cube = pltpu.VMEM((3, 4, 4, 4, BS, BS), jnp.bfloat16)
    dma = pltpu.SemaphoreType.DMA
    return pl.pallas_call(
        return_kernel,
        out_shape=[
            jax.ShapeDtypeStruct((3, 4, 4, 4, BS, BS), jnp.bfloat16),
            jax.ShapeDtypeStruct((3, 2 * CAP, BS, BS), jnp.bfloat16),
        ],
        in_specs=[smem, hbm],
        out_specs=[hbm, hbm],
        scratch_shapes=[cube, cube]
        + [pltpu.VMEM((4, 4, 4, BS, BS), jnp.bfloat16)] * 3
        + [pltpu.VMEM((3, 2 * CAP, BS, BS), jnp.bfloat16)]
        + [dma((3, 2)), dma((3, 2)), dma((3, 3, 3)), dma((3, 3, 3)), dma((3, 3)), dma((3,))],
        compiler_params=pltpu.CompilerParams(
            collective_id=2, has_side_effects=True, vmem_limit_bytes=50 * 2**20
        ),
        name="return_pieces",
    )(tab, pieces)


def collect_kernel(half, place, tab, got, back, *rest):
    if half:
        out, total, got_v, back_v, sems = rest
    else:
        part, out, got_v, back_v, sems = rest
        total = out
    c = place[3]
    loads = []
    for k in range(3):
        loads.append(
            (
                pltpu.make_async_copy(got.at[k], got_v.at[k], sems.at[0, k]),
                pltpu.make_async_copy(back.at[k], back_v.at[k], sems.at[1, k]),
            )
        )
        start_all(loads[k])
    total[...] = jnp.zeros_like(total) if half else part[...].astype(jnp.float32)

    def put(index, block):
        index = index - 72 * half

        @pl.when((index >= 0) & (index < 72))
        def _():
            total[jnp.clip(index, 0, 71)] += block().astype(jnp.float32)

    for k in range(3):
        wait_all(loads[k])

        def add(i, cc, k=k):
            for n in range(4):
                put(tab[k, 8 * i + 2 * n + c], lambda: got_v[k, 4 * i + n])
            return cc

        lax.fori_loop(0, 16, add, 0)

        def add_back(j, cc, k=k):
            for side in range(2):
                put(tab[8 + j, 3 * side + k], lambda: back_v[k, side * CAP + j])
            return cc

        lax.fori_loop(0, CAP, add_back, 0)
    if half:
        out[...] = total[...].astype(jnp.bfloat16)


def collect(half, place, tab, got, back, *part):
    smem = pl.BlockSpec(memory_space=pltpu.SMEM)
    vmem = pl.BlockSpec(memory_space=pltpu.VMEM)
    hbm = pl.BlockSpec(memory_space=pl.ANY)
    return pl.pallas_call(
        functools.partial(collect_kernel, half),
        out_shape=jax.ShapeDtypeStruct((72, BS, BS), jnp.bfloat16 if half else jnp.float32),
        in_specs=[smem, smem, hbm, hbm] + [vmem] * len(part),
        out_specs=vmem,
        scratch_shapes=([pltpu.VMEM((72, BS, BS), jnp.float32)] if half else [])
        + [
            pltpu.VMEM((3, 64, BS, BS), jnp.bfloat16),
            pltpu.VMEM((3, 2 * CAP, BS, BS), jnp.bfloat16),
            pltpu.SemaphoreType.DMA((2, 3)),
        ],
        compiler_params=pltpu.CompilerParams(vmem_limit_bytes=50 * 2**20),
        name="collect_sibling" if half else "collect_own",
    )(place, tab, got.reshape(3, 64, BS, BS), back, *part)


def swap_cores(value):
    return lax.ppermute(value, "bulk", [(i, i ^ 1) for i in range(32)])


def fast_path(density, factors, core, mine, sibling, tables, place, tab, coul):
    recv = fetch_blocks(tab, density, sibling).reshape(192, BS, BS)
    pieces = compute(mine, tab, tables, core, coul, recv, factors, 192)
    got, back = return_pieces(tab, pieces.reshape(3, 4, 4, 4, BS, BS))
    part = swap_cores(collect(1, place, tab, got, back))
    return collect(0, place, tab, got, back, part).reshape(24, 3, BS, BS)


def column_of(ids, d, bulk):
    group = bulk // 8
    local = jnp.int32(-1)
    for j in range(3):
        block = ids[d * T + group * 3 + j]
        local = jnp.where(block // 3 == bulk, block % 3, local)
    return local


def pack_kernel(place, ids, density, out, sem):
    row = place[0]
    bulk = place[1]

    def copy(d, j, col):
        r = ids[d * T + row * 3 + j] - row * 24
        return pltpu.make_async_copy(density.at[r, col], out.at[d * 3 + j], sem)

    def send(d, n):
        col = column_of(ids, d, bulk)

        @pl.when(col >= 0)
        def _():
            for j in range(3):
                copy(d, j, col).start()

        return n + (col >= 0).astype(jnp.int32)

    n = lax.fori_loop(0, 128, send, 0)

    def drain(i, c):
        pltpu.make_async_copy(out.at[pl.ds(0, 3)], out.at[pl.ds(0, 3)], sem).wait()
        return c

    lax.fori_loop(0, n, drain, 0)


def pack(place, ids, density):
    smem = pl.BlockSpec(memory_space=pltpu.SMEM)
    hbm = pl.BlockSpec(memory_space=pl.ANY)
    return pl.pallas_call(
        pack_kernel,
        out_shape=jax.ShapeDtypeStruct((384, BS, BS), jnp.bfloat16),
        in_specs=[smem, smem, hbm],
        out_specs=hbm,
        scratch_shapes=[pltpu.SemaphoreType.DMA],
        name="pack_density",
    )(place, ids, density)


def gather_kernel(place, ids, inbound, fock, buf, sems):
    row = place[0]
    bulk = place[1]

    def fetch(d, c):
        @pl.when(column_of(ids, d, bulk) >= 0)
        def _():
            pltpu.make_async_copy(inbound.at[pl.ds(d * 3, 3)], buf.at[pl.ds(d * 3, 3)], sems.at[d]).start()

        return c

    lax.fori_loop(0, 128, fetch, 0)
    fock[...] = jnp.zeros_like(fock)

    def add(d, c):
        col = column_of(ids, d, bulk)

        @pl.when(col >= 0)
        def _():
            pltpu.make_async_copy(inbound.at[pl.ds(d * 3, 3)], buf.at[pl.ds(d * 3, 3)], sems.at[d]).wait()
            for j in range(3):
                r = ids[d * T + row * 3 + j] - row * 24
                fock[r, col] += buf[d * 3 + j].astype(jnp.float32)

        return c

    lax.fori_loop(0, 128, add, 0)


def gather(place, ids, inbound):
    smem = pl.BlockSpec(memory_space=pltpu.SMEM)
    vmem = pl.BlockSpec(memory_space=pltpu.VMEM)
    hbm = pl.BlockSpec(memory_space=pl.ANY)
    return pl.pallas_call(
        gather_kernel,
        out_shape=jax.ShapeDtypeStruct((24, 3, BS, BS), jnp.float32),
        in_specs=[smem, smem, hbm],
        out_specs=vmem,
        scratch_shapes=[pltpu.VMEM((384, BS, BS), jnp.bfloat16), pltpu.SemaphoreType.DMA((128,))],
        compiler_params=pltpu.CompilerParams(vmem_limit_bytes=40 * 2**20),
        name="add_pieces",
    )(place, ids, inbound)


def slow_path(density, factors, core, mine, tables, place, tab, ids, coul):
    axes = ("row", "bulk")
    where = jnp.stack([place[0], place[1] * 8 + place[2] * 2 + place[3]])
    ids = ids[:, :T].reshape(-1)
    sent = pack(where, ids, density)
    recv = lax.all_to_all(sent, axes, split_axis=0, concat_axis=0, tiled=True)
    owner = mine[:, None] // 24 * 32 + mine[None, :] // 3
    slot = (owner * 3 + (jnp.arange(T) % 3)[:, None]).reshape(-1)
    pieces = compute(mine, tab, tables, core, coul, recv[slot], factors, NP, direct=True)
    outbound = jnp.zeros((384, BS, BS), jnp.bfloat16).at[slot].set(pieces)
    inbound = lax.all_to_all(outbound, axes, split_axis=0, concat_axis=0, tiled=True)
    return gather(where, ids, inbound)


def shards(density, factors, core, task_blocks, quartets, quartet_count):
    mine = task_blocks[0]
    bulk = lax.axis_index("bulk")
    place = jnp.stack([lax.axis_index("row"), bulk // 8, bulk // 2 % 4, bulk % 2]).astype(jnp.int32)
    ids, sibling = share_tasks(task_blocks, density)
    tables, coul = entries(quartets, quartet_count)
    tab = route(place, ids)
    fock = fast_path(density, factors, core, mine, sibling, tables, place, tab, coul)

    def again(state):
        return state[0]

    def padded(state):
        return jnp.array(False), slow_path(density, factors, core, mine, tables, place, tab, ids, coul)

    return lax.while_loop(again, padded, (tab[7, 127] > 0, fock))[1]


def solution(mesh):
    return jax.shard_map(
        shards,
        mesh=mesh,
        in_specs=(
            P("row", "bulk", None, None),
            P(),
            P(),
            P(("row", "bulk"), None),
            P(("row", "bulk"), None),
            P(("row", "bulk")),
        ),
        out_specs=P("row", "bulk", None, None),
        check_vma=False,
    )
```
